256 devices in a mesh: dp: 32 (over y, z), tensor: 8 (over x, core).
Axes of the slice: x: 4, y: 4, z: 8, core: 2. Of those that a mesh axis runs over, the one named last changes fastest.
Arguments:
- momentum: float32 [8192, 14336], P('dp', 'tensor'), may hold values from -6 to 6
- gradient: bfloat16 [8192, 14336], P('dp', 'tensor'), may hold values from -120 to 120
- factor: bfloat16 [14336, 512], P('tensor'), may hold values from -6 to 6
- weight: bfloat16 [8192, 14336], P('dp', 'tensor'), may hold values from -6 to 6
Outputs:
- new_momentum: float32 [8192, 14336], P('dp', 'tensor')
- new_factor: bfloat16 [14336, 512], P('tensor')
- new_weight: bfloat16 [8192, 14336], P('dp', 'tensor')
The draws below stay inside these ranges and needn't reach their ends.
All inputs are finite; a program needn't handle non-finite values.
Results may differ from the reference program's by a relative error of at most 0.0027.
Values may be sent and summed in bfloat16 or wider, within the bound.
No kernel may reach another device: no remote copies, remote signals or barrier semaphores. Data moves between devices by JAX's collectives and lax.ppermute only.
A program may use at most 64 MiB of HBM per device.

```python
import math
import jax
import jax.numpy as jnp
from jax import lax

D = 8192
N = 14336
RANK = 512


def draw_gradient(key, part):
    key = jax.random.fold_in(key, 7)
    base_key, row_key, col_key = jax.random.split(key, 3)
    row_pos = jnp.arange(D, dtype=jnp.float32) / D
    col_pos = jnp.arange(N, dtype=jnp.float32) / N
    row_noise = jax.random.uniform(row_key, (D,), jnp.float32)
    col_noise = jax.random.uniform(col_key, (N,), jnp.float32)
    values = jnp.clip(jax.random.normal(base_key, (D, N), jnp.float32), -4.0, 4.0)
    row_scale = jnp.exp(math.log(10.0) * (0.5 * row_pos + 0.5 * row_noise))
    col_scale = jnp.exp(math.log(10.0) * (0.5 * col_pos + 0.5 * col_noise))
    return (0.3 * values * row_scale[:, None] * col_scale[None, :]).astype(jnp.bfloat16)


def level_of(key, shape, shards, low, largest):
    def one(position, parts):
        heights = jax.random.uniform(jax.random.fold_in(jax.random.fold_in(key, 6), position), (parts,), jnp.float32, low / len(shards), largest / len(shards))
        return jnp.repeat(jnp.exp(heights), shape[position] // parts).reshape((-1,) + (1,) * (len(shape) - position - 1))

    factor_of = one(*shards[0])
    for cut in shards[1:]:
        factor_of = factor_of * one(*cut)
    return factor_of


def centred(own_key, dims, scale, limit, cuts=(), kind=jnp.bfloat16):
    values = jax.random.normal(own_key, dims, jnp.float32) * scale
    if len(cuts) > 0:
        values = level_of(own_key, dims, cuts, -0.22, 0.18) * values
    return jnp.clip(values, min=-limit, max=limit).astype(kind)


def setup_inputs(seed: int = 0) -> dict:
    key_of = jax.random.split(jax.random.key(seed), 5)
    momentum = centred(key_of[0], (D, N), 1.0, 6.0, ((0, 32), (1, 8)), jnp.float32)
    gradient = draw_gradient(jax.random.fold_in(key_of[4], 71), 0)
    factor = centred(key_of[2], (N, RANK), 1.0, 6.0, ((0, 8),))
    weight = centred(key_of[3], (D, N), 1.0, 6.0, ((0, 32), (1, 8)))
    return {"momentum": momentum, "gradient": gradient, "factor": factor, "weight": weight}


precise = lax.Precision.HIGHEST
decay_rate = 0.95
learn_rate = 0.5
epsilon = 1e-06

def reference(momentum, gradient, factor, weight):
    combined = momentum + gradient.astype(jnp.float32)
    projected = jnp.dot(combined, factor.astype(jnp.float32), precision=precise)
    gram = jnp.dot(projected.T, projected, precision=precise)
    lower_factor = jnp.linalg.cholesky(gram)
    basis = jax.scipy.linalg.solve_triangular(lower_factor, projected.T, lower=True).T
    right = jnp.dot(combined.T, basis, precision=precise)
    col_scale = jnp.sqrt(lax.optimization_barrier(jnp.mean(right * right, axis=0)) + epsilon)
    new_factor = (right / col_scale).astype(jnp.bfloat16)
    factor_wide = new_factor.astype(jnp.float32)
    direction = jnp.dot(basis, factor_wide.T, precision=precise)
    feedback = jnp.dot(basis * col_scale, factor_wide.T, precision=precise)
    new_momentum = combined - (1.0 - decay_rate) * feedback
    step_size = learn_rate * (D / RANK) ** 0.5
    new_weight = (weight.astype(jnp.float32) - step_size * direction).astype(jnp.bfloat16)
    return (new_momentum, new_factor, new_weight)
```

```python
import functools

import jax
import jax.numpy as jnp
from jax import lax
from jax.experimental import pallas as pl
from jax.experimental.pallas import tpu as pltpu
from jax.sharding import PartitionSpec as P

D = 8192
RANK = 512
BLOCK = 128
BLOCKS = RANK // BLOCK
UPPER = [(i, j) for i in range(BLOCKS) for j in range(i, BLOCKS)]
NY, NZ, NX = 4, 8, 4

precise = lax.Precision.HIGHEST
decay_rate = 0.95
learn_rate = 0.5
epsilon = 1e-06
f32 = jnp.float32
bf16 = jnp.bfloat16

Z_GROUPS = [[y * NZ + z for z in range(NZ)] for y in range(NY)]


def from_y(k):
    return [((i + NZ * k) % (NY * NZ), i) for i in range(NY * NZ)]


def from_z(k):
    return [(i // NZ * NZ + (i + k) % NZ, i) for i in range(NY * NZ)]


def from_x(k):
    return [((i + 2 * k) % (2 * NX), i) for i in range(2 * NX)]


OTHER_CORE = [(i ^ 1, i) for i in range(2 * NX)]


def sublane(v, i):
    return jnp.broadcast_to(v[i : i + 1, :], (8, BLOCK))


def column(v, c):
    return jnp.broadcast_to(v[:, c : c + 1], (8, BLOCK))


def invert_factor(a):
    lane = lax.broadcasted_iota(jnp.int32, (8, BLOCK), 1)
    sub = lax.broadcasted_iota(jnp.int32, (8, BLOCK), 0)
    out = []
    for p in range(16):
        r = a[p]
        here = (lane >= 8 * p) & (lane < 8 * p + 8)
        cols = [column(r, 8 * p + k) for k in range(8)]
        r = jnp.where(here, jnp.where(lane == sub + 8 * p, 1.0, 0.0), r)
        x = jnp.zeros((8, BLOCK), f32)
        for j in range(8):
            pivot_col = cols[j]
            pivot = sublane(pivot_col, j)
            recip = 1.0 / pivot
            at = sub == j

            def eliminate(v, pivot_col=pivot_col, recip=recip, at=at, j=j):
                row = sublane(v, j) * recip
                return jnp.where(at, row, v - pivot_col * row)

            for k in range(j + 1, 8):
                cols[k] = eliminate(cols[k])
            x = jnp.where(at, sublane(r, j) * lax.rsqrt(pivot), x)
            r = eliminate(r)
        out.append(jnp.where(lane <= sub + 8 * p, x, 0.0))
        rows = [sublane(r, j) for j in range(8)]
        for q in range(p + 1, 16):
            v = a[q]
            t = [column(v, 8 * p + j) * rows[j] for j in range(8)]
            total = ((t[0] + t[1]) + (t[2] + t[3])) + ((t[4] + t[5]) + (t[6] + t[7]))
            a[q] = jnp.where(here, 0.0, v) - total
    return out


def cholesky_kernel(g_ref, x_ref, z_ref, t_ref):
    z_ref[...] = jnp.zeros_like(z_ref)
    for n, (i, j) in enumerate(UPPER):
        z_ref[i * BLOCK : (i + 1) * BLOCK, j * BLOCK : (j + 1) * BLOCK] = g_ref[n * BLOCK : (n + 1) * BLOCK, :]
    col_block = lax.broadcasted_iota(jnp.int32, (RANK, RANK), 1) // BLOCK
    row_cols = lax.broadcasted_iota(jnp.int32, (BLOCK, RANK), 1) // BLOCK

    def step(b, carry):
        start = pl.multiple_of(b * BLOCK, BLOCK)
        a = [z_ref[pl.ds(pl.multiple_of(start + 8 * i, 8), 8), pl.ds(start, BLOCK)] for i in range(16)]
        for i, v in enumerate(invert_factor(a)):
            t_ref[8 * i : 8 * i + 8, :] = v
        t = t_ref[...]
        n = jnp.dot(t, z_ref[pl.ds(start, BLOCK), :], precision=precise, preferred_element_type=f32)
        n = jnp.where(row_cols == b, jnp.concatenate([t] * BLOCKS, axis=1), n)
        x_ref[pl.ds(start, BLOCK), :] = jnp.where(row_cols <= b, n, 0.0)
        m = jnp.where(row_cols > b, n, 0.0)
        update = lax.dot_general(m, n, (((0,), (0,)), ((), ())), precision=precise, preferred_element_type=f32)
        z_ref[...] = jnp.where(col_block == b, 0.0, z_ref[...]) - update
        return carry

    lax.fori_loop(0, BLOCKS, step, 0)


def inverse_cholesky(packed):
    return pl.pallas_call(
        cholesky_kernel,
        out_shape=jax.ShapeDtypeStruct((RANK, RANK), f32),
        in_specs=[pl.BlockSpec(memory_space=pltpu.VMEM)],
        out_specs=pl.BlockSpec(memory_space=pltpu.VMEM),
        scratch_shapes=[pltpu.VMEM((RANK, RANK), f32), pltpu.VMEM((BLOCK, BLOCK), f32)],
        compiler_params=pltpu.CompilerParams(vmem_limit_bytes=24 * 1024 * 1024),
        cost_estimate=pl.CostEstimate(flops=6 * RANK**3, bytes_accessed=2 * 4 * RANK**2, transcendentals=0),
    )(packed)


def dot(a, b):
    return jnp.dot(a, b, precision=precise)


def dot_t(a, b):
    return lax.dot_general(a, b, (((1,), (1,)), ((), ())), precision=precise)


def split2(a):
    hi = a.astype(bf16)
    lo = (a - hi.astype(f32)).astype(bf16)
    return hi, lo


def rolled(parts, shift):
    n, rows = len(parts), parts[0].shape[0]
    twice = jnp.concatenate(parts + parts, axis=0)
    return lax.dynamic_slice_in_dim(twice, ((n - shift) % n) * rows, n * rows, 0)


def both_cores(core, mine, other):
    return jnp.where(core == 0, jnp.concatenate([mine, other], 0), jnp.concatenate([other, mine], 0))


def shards(momentum, gradient, factor, weight):
    dp, tp = lax.axis_index("dp"), lax.axis_index("tensor")
    core = tp % 2
    y, z = dp // NZ, dp % NZ
    rows, cols = momentum.shape
    half, quarter = rows // 2, cols // NY
    eighth = quarter // NZ

    combined = momentum + gradient.astype(f32)
    proj_part = dot(combined, factor.astype(f32))
    flipped = combined.T
    blocks = []
    for k in range(NY):
        block = lax.dynamic_slice_in_dim(flipped, ((y - k) % NY) * quarter, quarter, 0)
        blocks.append(block if k == 0 else lax.ppermute(block, "dp", from_y(k)))

    given = lax.dynamic_slice_in_dim(proj_part, (1 - core) * half, half, 0)
    kept = lax.dynamic_slice_in_dim(proj_part, core * half, half, 0)
    pair = kept + lax.ppermute(given, "tensor", OTHER_CORE)
    xs = [pair] + [lax.ppermute(pair, "tensor", from_x(k)) for k in range(1, NX)]
    mine = (xs[0] + xs[2]) + (xs[1] + xs[3])
    mine_y = [mine] + [lax.ppermute(mine, "dp", from_y(k)) for k in range(1, NY)]
    mine_all = jnp.concatenate(mine_y, 0)
    other_all = lax.ppermute(mine_all, "tensor", OTHER_CORE)

    right0 = None
    projected = None
    for k in range(NY):
        full = both_cores(core, mine_all[k * half : (k + 1) * half], other_all[k * half : (k + 1) * half])
        term = dot(blocks[k], full)
        right0 = term if k == 0 else right0 + term
        if k == 0:
            projected = full
    right0_part = lax.psum_scatter(right0, "dp", axis_index_groups=Z_GROUPS, tiled=True)

    gram = lax.dot_general(mine_all, mine_all, (((0,), (0,)), ((), ())), precision=precise)
    packed = jnp.concatenate([gram[i * BLOCK : (i + 1) * BLOCK, j * BLOCK : (j + 1) * BLOCK] for i, j in UPPER], 0)
    few = packed.shape[0] // 2
    gram_given = lax.dynamic_slice_in_dim(packed, (1 - core) * few, few, 0)
    gram_kept = lax.dynamic_slice_in_dim(packed, core * few, few, 0)
    gram_pair = gram_kept + lax.ppermute(gram_given, "tensor", OTHER_CORE)
    swapped = lax.all_to_all(gram_pair, "dp", 0, 0, axis_index_groups=Z_GROUPS, tiled=True)
    gram_part = jnp.sum(swapped.reshape(NZ, few // NZ, BLOCK), axis=0)
    gram_half = lax.all_to_all(jnp.concatenate([gram_part] * NZ, 0), "dp", 0, 0, axis_index_groups=Z_GROUPS, tiled=True)
    gram_all = both_cores(core, gram_half, lax.ppermute(gram_half, "tensor", OTHER_CORE))

    right0_z = [right0_part] + [lax.ppermute(right0_part, "dp", from_z(k)) for k in range(1, NZ)]
    inverse = inverse_cholesky(gram_all)
    right0_quarter = rolled(right0_z, z)

    right = dot_t(right0_quarter, inverse)
    squares = jnp.sum(right * right, axis=0, keepdims=True)

    def level(s):
        return jnp.sqrt(jnp.maximum(s / quarter, 1e-30))

    sent = (right / level(squares)).astype(jnp.float16)
    sent_y = [sent] + [lax.ppermute(sent, "dp", from_y(k)) for k in range(1, NY)]
    squares_y = [squares] + [lax.ppermute(squares, "dp", from_y(k)) for k in range(1, NY)]
    total = (squares_y[0] + squares_y[2]) + (squares_y[1] + squares_y[3])
    total_x = [total] + [lax.ppermute(total, "tensor", from_x(k)) for k in range(1, NX)]
    total = (total_x[0] + total_x[2]) + (total_x[1] + total_x[3])
    total = total + lax.ppermute(total, "tensor", OTHER_CORE)
    scale = jnp.sqrt(total / (cols * 2 * NX) + epsilon)

    basis = dot_t(projected, inverse)
    parts = [(s.astype(f32) * level(q) / scale).astype(bf16) for s, q in zip(sent_y, squares_y)]
    new_factor = rolled(parts, y)

    def times_factor(a):
        hi, lo = split2(a)
        one = functools.partial(lax.dot_general, dimension_numbers=(((1,), (1,)), ((), ())), preferred_element_type=f32)
        return one(hi, new_factor) + one(lo, new_factor)

    new_momentum = combined - (1.0 - decay_rate) * times_factor(basis * scale)
    step_size = learn_rate * (D / RANK) ** 0.5
    new_weight = (weight.astype(f32) - step_size * times_factor(basis)).astype(bf16)
    return new_momentum, new_factor, new_weight


def solution(mesh):
    in_specs = (P("dp", "tensor"), P("dp", "tensor"), P("tensor", None), P("dp", "tensor"))
    out_specs = (P("dp", "tensor"), P("tensor", None), P("dp", "tensor"))
    return jax.shard_map(shards, mesh=mesh, in_specs=in_specs, out_specs=out_specs, check_vma=False)
```

```python
import functools

import jax
import jax.numpy as jnp
from jax import lax
from jax.experimental import pallas as pl
from jax.experimental.pallas import tpu as pltpu
from jax.sharding import PartitionSpec as P

D = 8192
RANK = 512
BLOCK = 128
BLOCKS = RANK // BLOCK
UPPER = [(i, j) for i in range(BLOCKS) for j in range(i, BLOCKS)]
NY, NZ, NX = 4, 8, 4

precise = lax.Precision.HIGHEST
decay_rate = 0.95
learn_rate = 0.5
epsilon = 1e-06
f32 = jnp.float32
bf16 = jnp.bfloat16

WIDE = 896
VMEM_LIMIT = 20 * 1024 * 1024
VMEM_ALL = 60 * 1024 * 1024

Y_GROUPS = [[y * NZ + z for y in range(NY)] for z in range(NZ)]
Z_GROUPS = [[y * NZ + z for z in range(NZ)] for y in range(NY)]


def from_y(k):
    return [((i + NZ * k) % (NY * NZ), i) for i in range(NY * NZ)]


def from_z(k):
    return [(i // NZ * NZ + (i + k) % NZ, i) for i in range(NY * NZ)]


def from_x(k):
    return [((i + 2 * k) % (2 * NX), i) for i in range(2 * NX)]


def to_neighbour(odd):
    return [(i, i // NZ * NZ + ((i % NZ + odd ^ 1) - odd) % NZ) for i in range(NY * NZ)]


OTHER_CORE = [(i ^ 1, i) for i in range(2 * NX)]


def sublane(v, i):
    return jnp.broadcast_to(v[i : i + 1, :], (8, BLOCK))


def column(v, c):
    return jnp.broadcast_to(v[:, c : c + 1], (8, BLOCK))


def invert_factor(a):
    lane = lax.broadcasted_iota(jnp.int32, (8, BLOCK), 1)
    sub = lax.broadcasted_iota(jnp.int32, (8, BLOCK), 0)
    out = []
    for p in range(16):
        r = a[p]
        here = (lane >= 8 * p) & (lane < 8 * p + 8)
        cols = [column(r, 8 * p + k) for k in range(8)]
        r = jnp.where(here, jnp.where(lane == sub + 8 * p, 1.0, 0.0), r)
        x = jnp.zeros((8, BLOCK), f32)
        for j in range(8):
            pivot_col = cols[j]
            pivot = sublane(pivot_col, j)
            recip = 1.0 / pivot
            at = sub == j

            def eliminate(v, pivot_col=pivot_col, recip=recip, at=at, j=j):
                row = sublane(v, j) * recip
                return jnp.where(at, row, v - pivot_col * row)

            for k in range(j + 1, 8):
                cols[k] = eliminate(cols[k])
            x = jnp.where(at, sublane(r, j) * lax.rsqrt(pivot), x)
            r = eliminate(r)
        out.append(jnp.where(lane <= sub + 8 * p, x, 0.0))
        rows = [sublane(r, j) for j in range(8)]
        for q in range(p + 1, 16):
            v = a[q]
            t = [column(v, 8 * p + j) * rows[j] for j in range(8)]
            total = ((t[0] + t[1]) + (t[2] + t[3])) + ((t[4] + t[5]) + (t[6] + t[7]))
            a[q] = jnp.where(here, 0.0, v) - total
    return out


def cholesky_steps(first, last, x_ref, z_ref, t_ref):
    col_block = lax.broadcasted_iota(jnp.int32, (RANK, RANK), 1) // BLOCK
    row_cols = lax.broadcasted_iota(jnp.int32, (BLOCK, RANK), 1) // BLOCK

    def step(b, carry):
        start = pl.multiple_of(b * BLOCK, BLOCK)
        a = [z_ref[pl.ds(pl.multiple_of(start + 8 * i, 8), 8), pl.ds(start, BLOCK)] for i in range(16)]
        for i, v in enumerate(invert_factor(a)):
            t_ref[8 * i : 8 * i + 8, :] = v
        t = t_ref[...]
        n = jnp.dot(t, z_ref[pl.ds(start, BLOCK), :], precision=precise, preferred_element_type=f32)
        n = jnp.where(row_cols == b, jnp.concatenate([t] * BLOCKS, axis=1), n)
        x_ref[pl.ds(start, BLOCK), :] = jnp.where(row_cols <= b, n, 0.0)
        m = jnp.where(row_cols > b, n, 0.0)
        update = lax.dot_general(m, n, (((0,), (0,)), ((), ())), precision=precise, preferred_element_type=f32)
        z_ref[...] = jnp.where(col_block == b, 0.0, z_ref[...]) - update
        return carry

    lax.fori_loop(first, last, step, 0)


def begin_kernel(place, mine_ref, other_ref, x_ref, z_ref, g_ref, t_ref):
    few = mine_ref.shape[0]
    core = place[0]
    g_ref[pl.ds(pl.multiple_of(core * few, few), few), :] = mine_ref[...]
    g_ref[pl.ds(pl.multiple_of((1 - core) * few, few), few), :] = other_ref[...]
    z_ref[...] = jnp.zeros_like(z_ref)
    for n, (i, j) in enumerate(UPPER):
        z_ref[i * BLOCK : (i + 1) * BLOCK, j * BLOCK : (j + 1) * BLOCK] = g_ref[n * BLOCK : (n + 1) * BLOCK, :]
    cholesky_steps(0, 1, x_ref, z_ref, t_ref)


def end_kernel(x_in, z_in, after, x_ref, z_ref, t_ref):
    z_ref[...] = z_in[...]
    x_ref[...] = x_in[...]
    cholesky_steps(1, BLOCKS, x_ref, z_ref, t_ref)


def begin_cholesky(place, mine, other):
    return call(
        begin_kernel,
        [shape((RANK, RANK))] * 2,
        [SMEM, VMEM, VMEM],
        [pltpu.VMEM((len(UPPER) * BLOCK, BLOCK), f32), pltpu.VMEM((BLOCK, BLOCK), f32)],
        40 * RANK**3,
        8 * RANK**2,
    )(place, mine, other)


def end_cholesky(half_done, rest, after):
    return call(
        end_kernel,
        [shape((RANK, RANK))],
        [VMEM, VMEM, pl.BlockSpec(memory_space=pl.ANY)],
        [pltpu.VMEM((RANK, RANK), f32), pltpu.VMEM((BLOCK, BLOCK), f32)],
        80 * RANK**3,
        8 * RANK**2,
    )(half_done, rest, after)[0]


SMEM = pl.BlockSpec(memory_space=pltpu.SMEM)
VMEM = pl.BlockSpec(memory_space=pltpu.VMEM)


def shape(dims, dtype=f32):
    return jax.ShapeDtypeStruct(dims, dtype)


def dot_t(a, b):
    return lax.dot_general(a, b, (((1,), (1,)), ((), ())), precision=precise, preferred_element_type=f32)


def dot_0(a, b):
    return lax.dot_general(a, b, (((0,), (0,)), ((), ())), precision=precise, preferred_element_type=f32)


def split3(a):
    hi = a.astype(bf16)
    rest = a - hi.astype(f32)
    mid = rest.astype(bf16)
    return hi, mid, (rest - mid.astype(f32)).astype(bf16)


def call(kernel, outs, ins, scratch, flops, moved):
    return pl.pallas_call(
        kernel,
        out_shape=outs,
        in_specs=ins,
        out_specs=[VMEM] * len(outs),
        scratch_shapes=scratch,
        compiler_params=pltpu.CompilerParams(vmem_limit_bytes=VMEM_LIMIT),
        cost_estimate=pl.CostEstimate(flops=flops, bytes_accessed=moved, transcendentals=0),
    )


def flip_kernel(momentum, gradient, flipped):
    flipped[...] = (momentum[...] + gradient[...].astype(f32)).T


def flip(momentum, gradient):
    rows, cols = momentum.shape
    block = pl.BlockSpec((rows, WIDE), lambda i: (0, i))
    return pl.pallas_call(
        flip_kernel,
        grid=(cols // WIDE,),
        out_shape=shape((cols, rows)),
        in_specs=[block, block],
        out_specs=pl.BlockSpec((WIDE, rows), lambda i: (i, 0)),
        compiler_params=pltpu.CompilerParams(vmem_limit_bytes=VMEM_ALL),
        cost_estimate=pl.CostEstimate(flops=0, bytes_accessed=10 * rows * cols, transcendentals=0),
    )(momentum, gradient)


def project_kernel(place, momentum, gradient, factor, given, kept, total):
    step, steps = pl.program_id(0), pl.num_programs(0)
    half = given.shape[0]
    hi, mid, lo = split3(momentum[...] + gradient[...].astype(f32))
    f = factor[...]
    part = (
        jnp.dot(lo, f, preferred_element_type=f32)
        + jnp.dot(mid, f, preferred_element_type=f32)
        + jnp.dot(hi, f, preferred_element_type=f32)
    )

    @pl.when(step == 0)
    def _():
        total[...] = part

    @pl.when(step > 0)
    def _():
        total[...] += part

    @pl.when(step == steps - 1)
    def _():
        core = place[0]
        given[...] = total[pl.ds(pl.multiple_of((1 - core) * half, half), half), :]
        kept[...] = total[pl.ds(pl.multiple_of(core * half, half), half), :]


def project(place, momentum, gradient, factor):
    rows, cols = momentum.shape
    wide = cols // 2
    outs = [shape((rows // 2, RANK))] * 2
    return pl.pallas_call(
        project_kernel,
        grid=(cols // wide,),
        out_shape=outs,
        in_specs=[
            SMEM,
            pl.BlockSpec((rows, wide), lambda i: (0, i)),
            pl.BlockSpec((rows, wide), lambda i: (0, i)),
            pl.BlockSpec((wide, RANK), lambda i: (i, 0)),
        ],
        out_specs=[pl.BlockSpec(s.shape, lambda i: (0, 0)) for s in outs],
        scratch_shapes=[pltpu.VMEM((rows, RANK), f32)],
        compiler_params=pltpu.CompilerParams(vmem_limit_bytes=VMEM_ALL),
        cost_estimate=pl.CostEstimate(flops=rows * cols, bytes_accessed=rows * cols, transcendentals=0),
    )(place, momentum, gradient, factor)


def gram_kernel(place, *refs):
    parts, (given, kept, stacked, packed) = refs[:NY], refs[NY:]
    half, few = parts[0].shape[0], given.shape[0]
    for k in range(NY):
        stacked[k * half : (k + 1) * half, :] = parts[k][...]
    n = 0
    for i in range(BLOCKS):
        strip = dot_0(stacked[:, i * BLOCK : (i + 1) * BLOCK], stacked[:, i * BLOCK :])
        for j in range(BLOCKS - i):
            packed[n * BLOCK : (n + 1) * BLOCK, :] = strip[:, j * BLOCK : (j + 1) * BLOCK]
            n += 1
    core = place[0]
    given[...] = packed[pl.ds(pl.multiple_of((1 - core) * few, few), few), :]
    kept[...] = packed[pl.ds(pl.multiple_of(core * few, few), few), :]


def gram_halves(place, parts):
    few = len(UPPER) * BLOCK // 2
    half = parts[0].shape[0]
    return call(
        gram_kernel,
        [shape((few, BLOCK))] * 2 + [shape((NY * half, RANK))],
        [SMEM] + [VMEM] * NY,
        [pltpu.VMEM((2 * few, BLOCK), f32)],
        12 * NY * half * RANK * RANK,
        4 * NY * half * RANK + 8 * few * BLOCK,
    )(place, *parts)


def share_kernel(swapped, out):
    rows = swapped.shape[0] // NZ
    terms = [swapped[k * rows : (k + 1) * rows, :] for k in range(NZ)]
    total = ((terms[0] + terms[1]) + (terms[2] + terms[3])) + ((terms[4] + terms[5]) + (terms[6] + terms[7]))
    for k in range(NZ):
        out[k * rows : (k + 1) * rows, :] = total


def share(swapped):
    return call(share_kernel, [shape(swapped.shape)], [VMEM], [], 0, 8 * swapped.size)(swapped)[0]


def right_kernel(place, mine, other, blocks, kept, given_a, given_b, projected, rows_all, cols_all, result):
    half = mine.shape[0] // NY
    eighth = result.shape[1]
    quarter = NZ * eighth
    core, odd = place[0], place[3]
    for k in range(NY):
        low = pl.multiple_of(2 * k * half + core * half, half)
        high = pl.multiple_of(2 * k * half + (1 - core) * half, half)
        rows_all[pl.ds(low, half), :] = mine[k * half : (k + 1) * half, :]
        rows_all[pl.ds(high, half), :] = other[k * half : (k + 1) * half, :]
        row = pl.multiple_of(lax.rem(place[1] + k, NY) * quarter, 8)
        cols_all[:, 2 * k * half : 2 * (k + 1) * half] = blocks[pl.ds(row, quarter), :]
    projected[...] = rows_all[: 2 * half, :]
    total = jnp.dot(cols_all[...], rows_all[...], precision=precise, preferred_element_type=f32)
    for s in range(NZ):
        result[s] = total[s * eighth : (s + 1) * eighth, :]
    for s in range(NZ // 2):
        kept[s] = result[2 * s + odd]
        given_a[s] = result[2 * s + 1 - odd, :, : RANK // 2]
        given_b[s] = result[2 * s + 1 - odd, :, RANK // 2 :]


def right_sums(place, mine, other, blocks):
    cols, rows = blocks.shape
    quarter = cols // NY
    eighth = quarter // NZ
    return call(
        right_kernel,
        [shape((NZ // 2, eighth, RANK))] + [shape((NZ // 2, eighth, RANK // 2))] * 2 + [shape((rows, RANK))],
        [SMEM] + [VMEM] * 3,
        [pltpu.VMEM((NY * rows, RANK), f32), pltpu.VMEM((quarter, NY * rows), f32), pltpu.VMEM((NZ, eighth, RANK), f32)],
        12 * quarter * NY * rows * RANK,
        4 * (quarter * NY * rows + NY * rows * RANK + quarter * RANK),
    )(place, mine, other, blocks)


def shift_kernel(place, kept, from_a, from_b, *outs):
    for k in range(NZ // 2):
        s = lax.rem(place[2] + 2 * k, NZ) // 2
        outs[k][:, : RANK // 2] = kept[s, :, : RANK // 2] + from_a[s]
        outs[k][:, RANK // 2 :] = kept[s, :, RANK // 2 :] + from_b[s]


def shifted(place, kept, from_a, from_b):
    eighth = kept.shape[1]
    return call(
        shift_kernel, [shape((eighth, RANK))] * (NZ // 2), [SMEM] + [VMEM] * 3, [], 0, 8 * kept.size
    )(place, kept, from_a, from_b)


def spread_kernel(a, b, c, d, out):
    total = (a[...] + c[...]) + (b[...] + d[...])
    rows = total.shape[0]
    for k in range(NZ):
        out[k * rows : (k + 1) * rows, :] = total


def spread_sum(parts):
    rows, cols = parts[0].shape
    return call(spread_kernel, [shape((NZ * rows, cols))], [VMEM] * len(parts), [], 0, 8 * NZ * rows * cols)(*parts)[0]


def level(squares, count):
    return jnp.sqrt(jnp.maximum(squares / count, 1e-30))


def normal_kernel(right0, inverse, sent, squares):
    right = dot_t(right0[...], inverse[...])
    sums = jnp.sum(right * right, axis=0, keepdims=True)
    squares[...] = sums
    sent[...] = right / level(sums, right.shape[0])


def normalised(right0, inverse):
    quarter = right0.shape[0]
    return call(
        normal_kernel,
        [shape((quarter, RANK)), shape((1, RANK))],
        [VMEM, VMEM],
        [],
        12 * quarter * RANK * RANK,
        8 * quarter * RANK,
    )(right0, inverse)


def update_kernel(place, momentum, gradient, weight, basis, scale, *refs):
    parts, squares = refs[:NY], refs[NY : 2 * NY]
    new_momentum, new_factor, new_weight, factor, spread = refs[2 * NY :]
    rows, wide = momentum.shape
    step = pl.program_id(0)
    quarter = parts[0].shape[0]

    @pl.when(step == 0)
    def _():
        s = scale[...]
        for k in range(NY):
            row = pl.multiple_of(lax.rem(place[1] + k, NY) * quarter, 64)
            factor[pl.ds(row, quarter), :] = (parts[k][...] * (level(squares[k][:1], quarter) / s)).astype(bf16)
        b = basis[...]
        for i, v in enumerate((b * s, b)):
            hi = v.astype(bf16)
            spread[2 * i * rows : (2 * i + 1) * rows, :] = hi
            spread[(2 * i + 1) * rows : (2 * i + 2) * rows, :] = (v - hi.astype(f32)).astype(bf16)

    f = factor[pl.ds(pl.multiple_of(step * wide, wide), wide), :]
    new_factor[...] = f
    products = lax.dot_general(spread[...], f, (((1,), (1,)), ((), ())), preferred_element_type=f32)

    def times(i):
        return products[2 * i * rows : (2 * i + 1) * rows] + products[(2 * i + 1) * rows : (2 * i + 2) * rows]

    combined = momentum[...] + gradient[...].astype(f32)
    new_momentum[...] = combined - (1.0 - decay_rate) * times(0)
    step_size = learn_rate * (D / RANK) ** 0.5
    new_weight[...] = (weight[...].astype(f32) - step_size * times(1)).astype(bf16)


def update(place, momentum, gradient, weight, basis, scale, parts, squares):
    rows, cols = momentum.shape
    block = pl.BlockSpec((rows, WIDE), lambda i: (0, i))
    whole = lambda a: pl.BlockSpec(a.shape, lambda i: (0, 0))
    return pl.pallas_call(
        update_kernel,
        grid=(cols // WIDE,),
        out_shape=[shape((rows, cols)), shape((cols, RANK), bf16), shape((rows, cols), bf16)],
        in_specs=[SMEM, block, block, block, whole(basis), whole(scale)] + [whole(a) for a in parts + squares],
        out_specs=[block, pl.BlockSpec((WIDE, RANK), lambda i: (i, 0)), block],
        scratch_shapes=[pltpu.VMEM((cols, RANK), bf16), pltpu.VMEM((4 * rows, RANK), bf16)],
        compiler_params=pltpu.CompilerParams(vmem_limit_bytes=40 * 1024 * 1024),
        cost_estimate=pl.CostEstimate(flops=8 * rows * cols * RANK, bytes_accessed=16 * rows * cols, transcendentals=0),
    )(place, momentum, gradient, weight, basis, scale, *parts, *squares)


def over_z(a):
    return lax.all_to_all(a, "dp", 0, 0, axis_index_groups=Z_GROUPS, tiled=True)


def shards(momentum, gradient, factor, weight):
    dp, tp = lax.axis_index("dp"), lax.axis_index("tensor")
    core, y, z = tp % 2, dp // NZ, dp % NZ
    place = jnp.stack([core, y, z, z % 2]).astype(jnp.int32)
    rows, cols = momentum.shape

    blocks = lax.all_to_all(flip(momentum, gradient), "dp", 0, 0, axis_index_groups=Y_GROUPS, tiled=True)
    given, kept = project(place, momentum, gradient, factor)
    pair = kept + lax.ppermute(given, "tensor", OTHER_CORE)
    xs = [pair] + [lax.ppermute(pair, "tensor", from_x(k)) for k in range(1, NX)]
    mine = (xs[0] + xs[2]) + (xs[1] + xs[3])
    mine, blocks = lax.optimization_barrier((mine, blocks))
    mine = [mine] + [lax.ppermute(mine, "dp", from_y(k)) for k in range(1, NY)]

    gram_given, gram_kept, mine = gram_halves(place, mine)
    gram_pair = gram_kept + lax.ppermute(gram_given, "tensor", OTHER_CORE)
    other = lax.ppermute(mine, "tensor", OTHER_CORE)

    gram_swapped = over_z(gram_pair)
    right_kept, right_a, right_b, projected = right_sums(place, mine, other, blocks)
    right_a = lax.ppermute(right_a, "dp", to_neighbour(0))
    right_b = lax.ppermute(right_b, "dp", to_neighbour(1))
    gram_half = over_z(share(gram_swapped))
    pairs = shifted(place, right_kept, right_a, right_b)
    pairs = [pairs[0]] + [lax.ppermute(pairs[k], "dp", from_z(NZ - 2 * k)) for k in range(1, NZ // 2)]
    gram_other = lax.ppermute(gram_half, "tensor", OTHER_CORE)
    half_done, rest = begin_cholesky(place, gram_half, gram_other)
    right0 = spread_sum(pairs)
    inverse = end_cholesky(half_done, rest, right0)
    right0 = over_z(right0)

    sent, squares = normalised(right0, inverse)
    sent = sent.astype(jnp.float16)
    sent_y = [sent] + [lax.ppermute(sent, "dp", from_y(k)) for k in range(1, NY)]
    squares_x = [squares] + [lax.ppermute(squares, "tensor", from_x(k)) for k in range(1, NX)]
    total = (squares_x[0] + squares_x[2]) + (squares_x[1] + squares_x[3])
    total = total + lax.ppermute(total, "tensor", OTHER_CORE)
    both = jnp.concatenate([squares, total], 0)
    both_y = [both] + [lax.ppermute(both, "dp", from_y(k)) for k in range(1, NY)]
    both_y, sent_y = lax.optimization_barrier((both_y, sent_y))
    total = (both_y[0][1:] + both_y[2][1:]) + (both_y[1][1:] + both_y[3][1:])
    scale = jnp.sqrt(total / (cols * 2 * NX) + epsilon)
    basis = dot_t(projected, inverse)
    sent_y = [a.astype(f32) for a in sent_y]
    return update(place, momentum, gradient, weight, basis, scale, sent_y, both_y)


def solution(mesh):
    in_specs = (P("dp", "tensor"), P("dp", "tensor"), P("tensor", None), P("dp", "tensor"))
    out_specs = (P("dp", "tensor"), P("tensor", None), P("dp", "tensor"))
    return jax.shard_map(shards, mesh=mesh, in_specs=in_specs, out_specs=out_specs, check_vma=False)
```

```python
import functools

import jax
import jax.numpy as jnp
from jax import lax
from jax.experimental import pallas as pl
from jax.experimental.pallas import tpu as pltpu
from jax.sharding import PartitionSpec as P

D = 8192
RANK = 512
BLOCK = 128
BLOCKS = RANK // BLOCK
UPPER = [(i, j) for i in range(BLOCKS) for j in range(i, BLOCKS)]
NY, NZ, NX = 4, 8, 4

precise = lax.Precision.HIGHEST
decay_rate = 0.95
learn_rate = 0.5
epsilon = 1e-06
f32 = jnp.float32
bf16 = jnp.bfloat16

WIDE = 896
VMEM_LIMIT = 20 * 1024 * 1024
VMEM_ALL = 60 * 1024 * 1024

Y_GROUPS = [[y * NZ + z for y in range(NY)] for z in range(NZ)]
Z_GROUPS = [[y * NZ + z for z in range(NZ)] for y in range(NY)]


def from_y(k):
    return [((i + NZ * k) % (NY * NZ), i) for i in range(NY * NZ)]


def from_z(k):
    return [(i // NZ * NZ + (i + k) % NZ, i) for i in range(NY * NZ)]


def from_x(k):
    return [((i + 2 * k) % (2 * NX), i) for i in range(2 * NX)]


def to_neighbour(odd):
    return [(i, i // NZ * NZ + ((i % NZ + odd ^ 1) - odd) % NZ) for i in range(NY * NZ)]


OTHER_CORE = [(i ^ 1, i) for i in range(2 * NX)]


def sublane(v, i):
    return jnp.broadcast_to(v[i : i + 1, :], (8, BLOCK))


def column(v, c):
    return jnp.broadcast_to(v[:, c : c + 1], (8, BLOCK))


def invert_factor(a):
    lane = lax.broadcasted_iota(jnp.int32, (8, BLOCK), 1)
    sub = lax.broadcasted_iota(jnp.int32, (8, BLOCK), 0)
    out = []
    for p in range(16):
        r = a[p]
        here = (lane >= 8 * p) & (lane < 8 * p + 8)
        cols = [column(r, 8 * p + k) for k in range(8)]
        r = jnp.where(here, jnp.where(lane == sub + 8 * p, 1.0, 0.0), r)
        x = jnp.zeros((8, BLOCK), f32)
        for j in range(8):
            pivot_col = cols[j]
            pivot = sublane(pivot_col, j)
            recip = 1.0 / pivot
            at = sub == j

            def eliminate(v, pivot_col=pivot_col, recip=recip, at=at, j=j):
                row = sublane(v, j) * recip
                return jnp.where(at, row, v - pivot_col * row)

            for k in range(j + 1, 8):
                cols[k] = eliminate(cols[k])
            x = jnp.where(at, sublane(r, j) * lax.rsqrt(pivot), x)
            r = eliminate(r)
        out.append(jnp.where(lane <= sub + 8 * p, x, 0.0))
        rows = [sublane(r, j) for j in range(8)]
        for q in range(p + 1, 16):
            v = a[q]
            t = [column(v, 8 * p + j) * rows[j] for j in range(8)]
            total = ((t[0] + t[1]) + (t[2] + t[3])) + ((t[4] + t[5]) + (t[6] + t[7]))
            a[q] = jnp.where(here, 0.0, v) - total
    return out


def cholesky_kernel(mine_ref, other_ref, after, x_ref, z_ref, g_ref, t_ref):
    few = mine_ref.shape[0]
    core = core_index()
    g_ref[pl.ds(pl.multiple_of(core * few, few), few), :] = mine_ref[...]
    g_ref[pl.ds(pl.multiple_of((1 - core) * few, few), few), :] = other_ref[...]
    for n, (i, j) in enumerate(UPPER):
        z_ref[i * BLOCK : (i + 1) * BLOCK, j * BLOCK : (j + 1) * BLOCK] = g_ref[n * BLOCK : (n + 1) * BLOCK, :]
    for b in range(BLOCKS):
        start, end = b * BLOCK, (b + 1) * BLOCK
        a = [z_ref[start + 8 * i : start + 8 * i + 8, start:end] for i in range(16)]
        for i, v in enumerate(invert_factor(a)):
            t_ref[8 * i : 8 * i + 8, :] = v
        t = t_ref[...]
        x_ref[start:end, start:end] = t
        if b > 0:
            x_ref[start:end, :start] = dot(t, z_ref[start:end, :start])
        if b < BLOCKS - 1:
            x_ref[start:end, end:] = jnp.zeros((BLOCK, RANK - end), f32)
            u = dot(t, z_ref[start:end, end:])
            lower = dot_0(u, x_ref[start:end, :end])
            if b > 0:
                z_ref[end:, :start] = z_ref[end:, :start] - lower[:, :start]
            z_ref[end:, start:end] = -lower[:, start:]
            for i in range(b + 1, BLOCKS):
                rows = slice(i * BLOCK, (i + 1) * BLOCK)
                own = u[:, i * BLOCK - end : (i + 1) * BLOCK - end]
                z_ref[rows, i * BLOCK :] = z_ref[rows, i * BLOCK :] - dot_0(own, u[:, i * BLOCK - end :])


def inverse_cholesky(mine, other, after):
    return call(
        cholesky_kernel,
        [shape((RANK, RANK))],
        [VMEM, VMEM, pl.BlockSpec(memory_space=pl.ANY)],
        [
            pltpu.VMEM((RANK, RANK), f32),
            pltpu.VMEM((len(UPPER) * BLOCK, BLOCK), f32),
            pltpu.VMEM((BLOCK, BLOCK), f32),
        ],
        80 * RANK**3,
        8 * RANK**2,
    )(mine, other, after)[0]


VMEM = pl.BlockSpec(memory_space=pltpu.VMEM)


def core_index():
    return lax.rem(lax.axis_index("tensor"), 2)


def y_index():
    return lax.axis_index("dp") // NZ


def z_index():
    return lax.rem(lax.axis_index("dp"), NZ)


def shape(dims, dtype=f32):
    return jax.ShapeDtypeStruct(dims, dtype)


def dot(a, b):
    return jnp.dot(a, b, precision=precise, preferred_element_type=f32)


def dot_t(a, b):
    return lax.dot_general(a, b, (((1,), (1,)), ((), ())), precision=precise, preferred_element_type=f32)


def dot_0(a, b):
    return lax.dot_general(a, b, (((0,), (0,)), ((), ())), precision=precise, preferred_element_type=f32)


def split3(a):
    hi = a.astype(bf16)
    rest = a - hi.astype(f32)
    mid = rest.astype(bf16)
    return hi, mid, (rest - mid.astype(f32)).astype(bf16)


def call(kernel, outs, ins, scratch, flops, moved):
    return pl.pallas_call(
        kernel,
        out_shape=outs,
        in_specs=ins,
        out_specs=[VMEM] * len(outs),
        scratch_shapes=scratch,
        compiler_params=pltpu.CompilerParams(vmem_limit_bytes=VMEM_LIMIT),
        cost_estimate=pl.CostEstimate(flops=flops, bytes_accessed=moved, transcendentals=0),
    )


def project_kernel(momentum, gradient, factor, flipped, given, kept, total, stacked):
    step, steps = pl.program_id(0), pl.num_programs(0)
    rows, half = momentum.shape[0], given.shape[0]
    combined = momentum[...] + gradient[...].astype(f32)
    flipped[...] = combined.T
    for i, v in enumerate(split3(combined)):
        stacked[i * rows : (i + 1) * rows, :] = v
    parts = jnp.dot(stacked[...], factor[...], preferred_element_type=f32)
    part = (parts[2 * rows :] + parts[rows : 2 * rows]) + parts[:rows]

    @pl.when(step == 0)
    def _():
        total[...] = part

    @pl.when(step > 0)
    def _():
        total[...] += part

    @pl.when(step == steps - 1)
    def _():
        core = core_index()
        given[...] = total[pl.ds(pl.multiple_of((1 - core) * half, half), half), :]
        kept[...] = total[pl.ds(pl.multiple_of(core * half, half), half), :]


def project(momentum, gradient, factor):
    rows, cols = momentum.shape
    half = shape((rows // 2, RANK))
    block = pl.BlockSpec((rows, WIDE), lambda i: (0, i))
    whole = pl.BlockSpec(half.shape, lambda i: (0, 0))
    return pl.pallas_call(
        project_kernel,
        grid=(cols // WIDE,),
        out_shape=[shape((cols, rows)), half, half],
        in_specs=[block, block, pl.BlockSpec((WIDE, RANK), lambda i: (i, 0))],
        out_specs=[pl.BlockSpec((WIDE, rows), lambda i: (i, 0)), whole, whole],
        scratch_shapes=[pltpu.VMEM((rows, RANK), f32), pltpu.VMEM((3 * rows, WIDE), bf16)],
        compiler_params=pltpu.CompilerParams(vmem_limit_bytes=VMEM_ALL),
        cost_estimate=pl.CostEstimate(flops=6 * rows * cols * RANK, bytes_accessed=10 * rows * cols, transcendentals=0),
    )(momentum, gradient, factor)


def gram_kernel(*refs):
    parts, (given, kept, stacked, packed) = refs[:NY], refs[NY:]
    half, few = parts[0].shape[0], given.shape[0]
    for k in range(NY):
        stacked[k * half : (k + 1) * half, :] = parts[k][...]
    n = 0
    for i in range(BLOCKS):
        strip = dot_0(stacked[:, i * BLOCK : (i + 1) * BLOCK], stacked[:, i * BLOCK :])
        for j in range(BLOCKS - i):
            packed[n * BLOCK : (n + 1) * BLOCK, :] = strip[:, j * BLOCK : (j + 1) * BLOCK]
            n += 1
    core = core_index()
    given[...] = packed[pl.ds(pl.multiple_of((1 - core) * few, few), few), :]
    kept[...] = packed[pl.ds(pl.multiple_of(core * few, few), few), :]


def gram_halves(parts):
    few = len(UPPER) * BLOCK // 2
    half = parts[0].shape[0]
    return call(
        gram_kernel,
        [shape((few, BLOCK))] * 2 + [shape((NY * half, RANK))],
        [VMEM] * NY,
        [pltpu.VMEM((2 * few, BLOCK), f32)],
        12 * NY * half * RANK * RANK,
        4 * NY * half * RANK + 8 * few * BLOCK,
    )(*parts)


def share_kernel(swapped, out):
    rows = swapped.shape[0] // NZ
    terms = [swapped[k * rows : (k + 1) * rows, :] for k in range(NZ)]
    total = ((terms[0] + terms[1]) + (terms[2] + terms[3])) + ((terms[4] + terms[5]) + (terms[6] + terms[7]))
    for k in range(NZ):
        out[k * rows : (k + 1) * rows, :] = total


def share(swapped):
    return call(share_kernel, [shape(swapped.shape)], [VMEM], [], 0, 8 * swapped.size)(swapped)[0]


def right_kernel(mine, other, blocks, kept, given_a, given_b, projected, rows_all, cols_all, result):
    half = mine.shape[0] // NY
    eighth = result.shape[1]
    quarter = NZ * eighth
    core, odd = core_index(), lax.rem(z_index(), 2)
    for k in range(NY):
        low = pl.multiple_of(2 * k * half + core * half, half)
        high = pl.multiple_of(2 * k * half + (1 - core) * half, half)
        rows_all[pl.ds(low, half), :] = mine[k * half : (k + 1) * half, :]
        rows_all[pl.ds(high, half), :] = other[k * half : (k + 1) * half, :]
        row = pl.multiple_of(lax.rem(y_index() + k, NY) * quarter, 8)
        cols_all[:, 2 * k * half : 2 * (k + 1) * half] = blocks[pl.ds(row, quarter), :]
    projected[...] = rows_all[: 2 * half, :]
    total = jnp.dot(cols_all[...], rows_all[...], precision=precise, preferred_element_type=f32)
    for s in range(NZ):
        result[s] = total[s * eighth : (s + 1) * eighth, :]
    for s in range(NZ // 2):
        kept[s] = result[2 * s + odd]
        given_a[s] = result[2 * s + 1 - odd, :, : RANK // 2]
        given_b[s] = result[2 * s + 1 - odd, :, RANK // 2 :]


def right_sums(mine, other, blocks):
    cols, rows = blocks.shape
    quarter = cols // NY
    eighth = quarter // NZ
    return call(
        right_kernel,
        [shape((NZ // 2, eighth, RANK))] + [shape((NZ // 2, eighth, RANK // 2))] * 2 + [shape((rows, RANK))],
        [VMEM] * 3,
        [pltpu.VMEM((NY * rows, RANK), f32), pltpu.VMEM((quarter, NY * rows), f32), pltpu.VMEM((NZ, eighth, RANK), f32)],
        12 * quarter * NY * rows * RANK,
        4 * (quarter * NY * rows + NY * rows * RANK + quarter * RANK),
    )(mine, other, blocks)


def shift_kernel(kept, from_a, from_b, *outs):
    for k in range(NZ // 2):
        s = lax.rem(z_index() + 2 * k, NZ) // 2
        outs[k][:, : RANK // 2] = kept[s, :, : RANK // 2] + from_a[s]
        outs[k][:, RANK // 2 :] = kept[s, :, RANK // 2 :] + from_b[s]


def shifted(kept, from_a, from_b):
    eighth = kept.shape[1]
    return call(
        shift_kernel, [shape((eighth, RANK))] * (NZ // 2), [VMEM] * 3, [], 0, 8 * kept.size
    )(kept, from_a, from_b)


def spread_kernel(a, b, c, d, out):
    total = (a[...] + c[...]) + (b[...] + d[...])
    rows = total.shape[0]
    for k in range(NZ):
        out[k * rows : (k + 1) * rows, :] = total


def spread_sum(parts):
    rows, cols = parts[0].shape
    return call(spread_kernel, [shape((NZ * rows, cols))], [VMEM] * len(parts), [], 0, 8 * NZ * rows * cols)(*parts)[0]


def level(squares, count):
    return jnp.sqrt(jnp.maximum(squares / count, 1e-30))


def normal_kernel(right0, inverse, sent, squares):
    right = dot_t(right0[...], inverse[...])
    sums = jnp.sum(right * right, axis=0, keepdims=True)
    squares[...] = sums
    sent[...] = right / level(sums, right.shape[0])


def normalised(right0, inverse):
    quarter = right0.shape[0]
    return call(
        normal_kernel,
        [shape((quarter, RANK)), shape((1, RANK))],
        [VMEM, VMEM],
        [],
        12 * quarter * RANK * RANK,
        8 * quarter * RANK,
    )(right0, inverse)


def update_kernel(momentum, gradient, weight, basis, scale, *refs):
    parts, squares = refs[:NY], refs[NY : 2 * NY]
    new_momentum, new_factor, new_weight, factor, spread = refs[2 * NY :]
    rows, wide = momentum.shape
    step = pl.program_id(0)
    quarter = parts[0].shape[0]

    @pl.when(step == 0)
    def _():
        s = scale[...]
        for k in range(NY):
            row = pl.multiple_of(lax.rem(y_index() + k, NY) * quarter, 64)
            factor[pl.ds(row, quarter), :] = (parts[k][...] * (level(squares[k][:1], quarter) / s)).astype(bf16)
        b = basis[...]
        for i, v in enumerate((b * s, b)):
            hi = v.astype(bf16)
            spread[2 * i * rows : (2 * i + 1) * rows, :] = hi
            spread[(2 * i + 1) * rows : (2 * i + 2) * rows, :] = (v - hi.astype(f32)).astype(bf16)

    f = factor[pl.ds(pl.multiple_of(step * wide, wide), wide), :]
    new_factor[...] = f
    products = lax.dot_general(spread[...], f, (((1,), (1,)), ((), ())), preferred_element_type=f32)

    def times(i):
        return products[2 * i * rows : (2 * i + 1) * rows] + products[(2 * i + 1) * rows : (2 * i + 2) * rows]

    combined = momentum[...] + gradient[...].astype(f32)
    new_momentum[...] = combined - (1.0 - decay_rate) * times(0)
    step_size = learn_rate * (D / RANK) ** 0.5
    new_weight[...] = (weight[...].astype(f32) - step_size * times(1)).astype(bf16)


def update(momentum, gradient, weight, basis, scale, parts, squares):
    rows, cols = momentum.shape
    block = pl.BlockSpec((rows, WIDE), lambda i: (0, i))
    whole = lambda a: pl.BlockSpec(a.shape, lambda i: (0, 0))
    return pl.pallas_call(
        update_kernel,
        grid=(cols // WIDE,),
        out_shape=[shape((rows, cols)), shape((cols, RANK), bf16), shape((rows, cols), bf16)],
        in_specs=[block, block, block, whole(basis), whole(scale)] + [whole(a) for a in parts + squares],
        out_specs=[block, pl.BlockSpec((WIDE, RANK), lambda i: (i, 0)), block],
        scratch_shapes=[pltpu.VMEM((cols, RANK), bf16), pltpu.VMEM((4 * rows, RANK), bf16)],
        compiler_params=pltpu.CompilerParams(vmem_limit_bytes=40 * 1024 * 1024),
        cost_estimate=pl.CostEstimate(flops=8 * rows * cols * RANK, bytes_accessed=16 * rows * cols, transcendentals=0),
    )(momentum, gradient, weight, basis, scale, *parts, *squares)


def over_z(a):
    return lax.all_to_all(a, "dp", 0, 0, axis_index_groups=Z_GROUPS, tiled=True)


def shards(momentum, gradient, factor, weight):
    rows, cols = momentum.shape

    flipped, given, kept = project(momentum, gradient, factor)
    blocks = lax.all_to_all(flipped, "dp", 0, 0, axis_index_groups=Y_GROUPS, tiled=True)
    pair = kept + lax.ppermute(given, "tensor", OTHER_CORE)
    xs = [pair] + [lax.ppermute(pair, "tensor", from_x(k)) for k in range(1, NX)]
    mine = (xs[0] + xs[2]) + (xs[1] + xs[3])
    mine = [mine] + [lax.ppermute(mine, "dp", from_y(k)) for k in range(1, NY)]
    mine, blocks = lax.optimization_barrier((mine, blocks))

    gram_given, gram_kept, stacked = gram_halves(mine)
    gram_pair = gram_kept + lax.ppermute(gram_given, "tensor", OTHER_CORE)
    other = lax.ppermute(stacked, "tensor", OTHER_CORE)

    right_kept, right_a, right_b, projected = right_sums(stacked, other, blocks)
    right_a = lax.ppermute(right_a, "dp", to_neighbour(0))
    right_b = lax.ppermute(right_b, "dp", to_neighbour(1))
    gram_shares = share(over_z(gram_pair))
    gram_shares, right_a, right_b = lax.optimization_barrier((gram_shares, right_a, right_b))
    pairs = shifted(right_kept, right_a, right_b)
    pairs = [pairs[0]] + [lax.ppermute(pairs[k], "dp", from_z(NZ - 2 * k)) for k in range(1, NZ // 2)]
    gram_half = over_z(gram_shares)
    gram_other = lax.ppermute(gram_half, "tensor", OTHER_CORE)
    right0 = spread_sum(pairs)
    inverse = inverse_cholesky(gram_half, gram_other, right0)
    right0 = over_z(right0)

    basis = dot_t(projected, inverse)
    basis, right0 = lax.optimization_barrier((basis, right0))
    sent, squares = normalised(right0, inverse)
    sent = sent.astype(jnp.float16)
    sent_y = [sent] + [lax.ppermute(sent, "dp", from_y(k)) for k in range(1, NY)]
    squares_x = [squares] + [lax.ppermute(squares, "tensor", from_x(k)) for k in range(1, NX)]
    total = (squares_x[0] + squares_x[2]) + (squares_x[1] + squares_x[3])
    total = total + lax.ppermute(total, "tensor", OTHER_CORE)
    both = jnp.concatenate([squares, total], 0)
    both_y = [both] + [lax.ppermute(both, "dp", from_y(k)) for k in range(1, NY)]
    both_y, sent_y = lax.optimization_barrier((both_y, sent_y))
    total = (both_y[0][1:] + both_y[2][1:]) + (both_y[1][1:] + both_y[3][1:])
    scale = jnp.sqrt(total / (cols * 2 * NX) + epsilon)
    sent_y = [a.astype(f32) for a in sent_y]
    return update(momentum, gradient, weight, basis, scale, sent_y, both_y)


def solution(mesh):
    in_specs = (P("dp", "tensor"), P("dp", "tensor"), P("tensor", None), P("dp", "tensor"))
    out_specs = (P("dp", "tensor"), P("tensor", None), P("dp", "tensor"))
    return jax.shard_map(shards, mesh=mesh, in_specs=in_specs, out_specs=out_specs, check_vma=False)
```

```python
import functools

import jax
import jax.numpy as jnp
from jax import lax
from jax.experimental import pallas as pl
from jax.experimental.pallas import tpu as pltpu
from jax.sharding import PartitionSpec as P

D = 8192
RANK = 512
BLOCK = 128
BLOCKS = RANK // BLOCK
UPPER = [(i, j) for i in range(BLOCKS) for j in range(i, BLOCKS)]
NY, NZ, NX = 4, 8, 4

precise = lax.Precision.HIGHEST
decay_rate = 0.95
learn_rate = 0.5
epsilon = 1e-06
f32 = jnp.float32
bf16 = jnp.bfloat16

WIDE = 896
VMEM_LIMIT = 20 * 1024 * 1024
VMEM_ALL = 60 * 1024 * 1024

Y_GROUPS = [[y * NZ + z for y in range(NY)] for z in range(NZ)]
Z_GROUPS = [[y * NZ + z for z in range(NZ)] for y in range(NY)]


def from_y(k):
    return [((i + NZ * k) % (NY * NZ), i) for i in range(NY * NZ)]


def from_z(k):
    return [(i // NZ * NZ + (i + k) % NZ, i) for i in range(NY * NZ)]


def from_x(k):
    return [((i + 2 * k) % (2 * NX), i) for i in range(2 * NX)]


def to_neighbour(odd):
    return [(i, i // NZ * NZ + ((i % NZ + odd ^ 1) - odd) % NZ) for i in range(NY * NZ)]


OTHER_CORE = [(i ^ 1, i) for i in range(2 * NX)]


def sublane(v, i):
    return jnp.broadcast_to(v[i : i + 1, :], (8, BLOCK))


def column(v, c):
    return jnp.broadcast_to(v[:, c : c + 1], (8, BLOCK))


def invert_factor(a):
    lane = lax.broadcasted_iota(jnp.int32, (8, BLOCK), 1)
    sub = lax.broadcasted_iota(jnp.int32, (8, BLOCK), 0)
    out = []
    for p in range(16):
        r = a[p]
        here = (lane >= 8 * p) & (lane < 8 * p + 8)
        cols = [column(r, 8 * p + k) for k in range(8)]
        r = jnp.where(here, jnp.where(lane == sub + 8 * p, 1.0, 0.0), r)
        x = jnp.zeros((8, BLOCK), f32)
        for j in range(8):
            pivot_col = cols[j]
            pivot = sublane(pivot_col, j)
            recip = 1.0 / pivot
            at = sub == j

            def eliminate(v, pivot_col=pivot_col, recip=recip, at=at, j=j):
                row = sublane(v, j) * recip
                return jnp.where(at, row, v - pivot_col * row)

            for k in range(j + 1, 8):
                cols[k] = eliminate(cols[k])
            x = jnp.where(at, sublane(r, j) * lax.rsqrt(pivot), x)
            r = eliminate(r)
        out.append(jnp.where(lane <= sub + 8 * p, x, 0.0))
        rows = [sublane(r, j) for j in range(8)]
        for q in range(p + 1, 16):
            v = a[q]
            t = [column(v, 8 * p + j) * rows[j] for j in range(8)]
            total = ((t[0] + t[1]) + (t[2] + t[3])) + ((t[4] + t[5]) + (t[6] + t[7]))
            a[q] = jnp.where(here, 0.0, v) - total
    return out


def cholesky_kernel(place, mine_ref, other_ref, after, x_ref, z_ref, g_ref, t_ref):
    few = mine_ref.shape[0]
    core = place[0]
    g_ref[pl.ds(pl.multiple_of(core * few, few), few), :] = mine_ref[...]
    g_ref[pl.ds(pl.multiple_of((1 - core) * few, few), few), :] = other_ref[...]
    for n, (i, j) in enumerate(UPPER):
        z_ref[i * BLOCK : (i + 1) * BLOCK, j * BLOCK : (j + 1) * BLOCK] = g_ref[n * BLOCK : (n + 1) * BLOCK, :]
    for b in range(BLOCKS):
        start, end = b * BLOCK, (b + 1) * BLOCK
        a = [z_ref[start + 8 * i : start + 8 * i + 8, start:end] for i in range(16)]
        for i, v in enumerate(invert_factor(a)):
            t_ref[8 * i : 8 * i + 8, :] = v
        t = t_ref[...]
        x_ref[start:end, start:end] = t
        if b > 0:
            x_ref[start:end, :start] = dot(t, z_ref[start:end, :start])
        if b < BLOCKS - 1:
            x_ref[start:end, end:] = jnp.zeros((BLOCK, RANK - end), f32)
            u = dot(t, z_ref[start:end, end:])
            lower = dot_0(u, x_ref[start:end, :end])
            if b > 0:
                z_ref[end:, :start] = z_ref[end:, :start] - lower[:, :start]
            z_ref[end:, start:end] = -lower[:, start:]
            for i in range(b + 1, BLOCKS):
                rows = slice(i * BLOCK, (i + 1) * BLOCK)
                own = u[:, i * BLOCK - end : (i + 1) * BLOCK - end]
                z_ref[rows, i * BLOCK :] = z_ref[rows, i * BLOCK :] - dot_0(own, u[:, i * BLOCK - end :])


def inverse_cholesky(place, mine, other, after):
    return call(
        cholesky_kernel,
        [shape((RANK, RANK))],
        [SMEM, VMEM, VMEM, ANY],
        [
            pltpu.VMEM((RANK, RANK), f32),
            pltpu.VMEM((len(UPPER) * BLOCK, BLOCK), f32),
            pltpu.VMEM((BLOCK, BLOCK), f32),
        ],
        80 * RANK**3,
        8 * RANK**2,
    )(place, mine, other, after)[0]


SMEM = pl.BlockSpec(memory_space=pltpu.SMEM)
VMEM = pl.BlockSpec(memory_space=pltpu.VMEM)
ANY = pl.BlockSpec(memory_space=pl.ANY)


def shape(dims, dtype=f32):
    return jax.ShapeDtypeStruct(dims, dtype)


def dot(a, b):
    return jnp.dot(a, b, precision=precise, preferred_element_type=f32)


def dot_t(a, b):
    return lax.dot_general(a, b, (((1,), (1,)), ((), ())), precision=precise, preferred_element_type=f32)


def dot_0(a, b):
    return lax.dot_general(a, b, (((0,), (0,)), ((), ())), precision=precise, preferred_element_type=f32)


def split3(a):
    hi = a.astype(bf16)
    rest = a - hi.astype(f32)
    mid = rest.astype(bf16)
    return hi, mid, (rest - mid.astype(f32)).astype(bf16)


def call(kernel, outs, ins, scratch, flops, moved):
    return pl.pallas_call(
        kernel,
        out_shape=outs,
        in_specs=ins,
        out_specs=[VMEM] * len(outs),
        scratch_shapes=scratch,
        compiler_params=pltpu.CompilerParams(vmem_limit_bytes=VMEM_LIMIT),
        cost_estimate=pl.CostEstimate(flops=flops, bytes_accessed=moved, transcendentals=0),
    )


def project_kernel(place, momentum, gradient, factor, flipped, given, kept, total, stacked):
    step, steps = pl.program_id(0), pl.num_programs(0)
    rows, half = momentum.shape[0], given.shape[0]
    combined = momentum[...] + gradient[...].astype(f32)
    flipped[...] = combined.T
    for i, v in enumerate(split3(combined)):
        stacked[i * rows : (i + 1) * rows, :] = v
    parts = jnp.dot(stacked[...], factor[...], preferred_element_type=f32)
    part = (parts[2 * rows :] + parts[rows : 2 * rows]) + parts[:rows]

    @pl.when(step == 0)
    def _():
        total[...] = part

    @pl.when(step > 0)
    def _():
        total[...] += part

    @pl.when(step == steps - 1)
    def _():
        core = place[0]
        given[...] = total[pl.ds(pl.multiple_of((1 - core) * half, half), half), :]
        kept[...] = total[pl.ds(pl.multiple_of(core * half, half), half), :]


def project(place, momentum, gradient, factor):
    rows, cols = momentum.shape
    half = shape((rows // 2, RANK))
    block = pl.BlockSpec((rows, WIDE), lambda i: (0, i))
    whole = pl.BlockSpec(half.shape, lambda i: (0, 0))
    return pl.pallas_call(
        project_kernel,
        grid=(cols // WIDE,),
        out_shape=[shape((cols, rows)), half, half],
        in_specs=[SMEM, block, block, pl.BlockSpec((WIDE, RANK), lambda i: (i, 0))],
        out_specs=[pl.BlockSpec((WIDE, rows), lambda i: (i, 0)), whole, whole],
        scratch_shapes=[pltpu.VMEM((rows, RANK), f32), pltpu.VMEM((3 * rows, WIDE), bf16)],
        compiler_params=pltpu.CompilerParams(vmem_limit_bytes=VMEM_ALL),
        cost_estimate=pl.CostEstimate(flops=6 * rows * cols * RANK, bytes_accessed=10 * rows * cols, transcendentals=0),
    )(place, momentum, gradient, factor)


def gram_kernel(place, *refs):
    parts, (after, given, kept, stacked, packed) = refs[:NY], refs[NY:]
    half, few = parts[0].shape[0], given.shape[0]
    for k in range(NY):
        stacked[k * half : (k + 1) * half, :] = parts[k][...]
    n = 0
    for i in range(BLOCKS):
        strip = dot_0(stacked[:, i * BLOCK : (i + 1) * BLOCK], stacked[:, i * BLOCK :])
        for j in range(BLOCKS - i):
            packed[n * BLOCK : (n + 1) * BLOCK, :] = strip[:, j * BLOCK : (j + 1) * BLOCK]
            n += 1
    core = place[0]
    given[...] = packed[pl.ds(pl.multiple_of((1 - core) * few, few), few), :]
    kept[...] = packed[pl.ds(pl.multiple_of(core * few, few), few), :]


def gram_halves(place, parts, after):
    few = len(UPPER) * BLOCK // 2
    half = parts[0].shape[0]
    return call(
        gram_kernel,
        [shape((few, BLOCK))] * 2 + [shape((NY * half, RANK))],
        [SMEM] + [VMEM] * NY + [ANY],
        [pltpu.VMEM((2 * few, BLOCK), f32)],
        12 * NY * half * RANK * RANK,
        4 * NY * half * RANK + 8 * few * BLOCK,
    )(place, *parts, after)


def share_kernel(swapped, out):
    rows = swapped.shape[0] // NZ
    terms = [swapped[k * rows : (k + 1) * rows, :] for k in range(NZ)]
    total = ((terms[0] + terms[1]) + (terms[2] + terms[3])) + ((terms[4] + terms[5]) + (terms[6] + terms[7]))
    for k in range(NZ):
        out[k * rows : (k + 1) * rows, :] = total


def share(swapped):
    return call(share_kernel, [shape(swapped.shape)], [VMEM], [], 0, 8 * swapped.size)(swapped)[0]


def right_kernel(place, mine, other, blocks, kept, given_a, given_b, projected, rows_all, cols_all, result):
    half = mine.shape[0] // NY
    eighth = result.shape[1]
    quarter = NZ * eighth
    core, odd = place[0], lax.rem(place[2], 2)
    for k in range(NY):
        low = pl.multiple_of(2 * k * half + core * half, half)
        high = pl.multiple_of(2 * k * half + (1 - core) * half, half)
        rows_all[pl.ds(low, half), :] = mine[k * half : (k + 1) * half, :]
        rows_all[pl.ds(high, half), :] = other[k * half : (k + 1) * half, :]
        row = pl.multiple_of(lax.rem(place[1] + k, NY) * quarter, 8)
        cols_all[:, 2 * k * half : 2 * (k + 1) * half] = blocks[pl.ds(row, quarter), :]
    projected[...] = rows_all[: 2 * half, :]
    total = jnp.dot(cols_all[...], rows_all[...], precision=precise, preferred_element_type=f32)
    for s in range(NZ):
        result[s] = total[s * eighth : (s + 1) * eighth, :]
    for s in range(NZ // 2):
        kept[s] = result[2 * s + odd]
        given_a[s] = result[2 * s + 1 - odd, :, : RANK // 2]
        given_b[s] = result[2 * s + 1 - odd, :, RANK // 2 :]


def right_sums(place, mine, other, blocks):
    cols, rows = blocks.shape
    quarter = cols // NY
    eighth = quarter // NZ
    return call(
        right_kernel,
        [shape((NZ // 2, eighth, RANK))] + [shape((NZ // 2, eighth, RANK // 2))] * 2 + [shape((rows, RANK))],
        [SMEM] + [VMEM] * 3,
        [pltpu.VMEM((NY * rows, RANK), f32), pltpu.VMEM((quarter, NY * rows), f32), pltpu.VMEM((NZ, eighth, RANK), f32)],
        12 * quarter * NY * rows * RANK,
        4 * (quarter * NY * rows + NY * rows * RANK + quarter * RANK),
    )(place, mine, other, blocks)


def shift_kernel(place, kept, from_a, from_b, *outs):
    for k in range(NZ // 2):
        s = lax.rem(place[2] + 2 * k, NZ) // 2
        outs[k][:, : RANK // 2] = kept[s, :, : RANK // 2] + from_a[s]
        outs[k][:, RANK // 2 :] = kept[s, :, RANK // 2 :] + from_b[s]


def shifted(place, kept, from_a, from_b):
    eighth = kept.shape[1]
    return call(
        shift_kernel, [shape((eighth, RANK))] * (NZ // 2), [SMEM] + [VMEM] * 3, [], 0, 8 * kept.size
    )(place, kept, from_a, from_b)


def spread_kernel(a, b, c, d, out):
    total = (a[...] + c[...]) + (b[...] + d[...])
    rows = total.shape[0]
    for k in range(NZ):
        out[k * rows : (k + 1) * rows, :] = total


def spread_sum(parts):
    rows, cols = parts[0].shape
    return call(spread_kernel, [shape((NZ * rows, cols))], [VMEM] * len(parts), [], 0, 8 * NZ * rows * cols)(*parts)[0]


def level(squares, count):
    return jnp.sqrt(jnp.maximum(squares / count, 1e-30))


def normal_kernel(right0, inverse, sent, squares):
    right = dot_t(right0[...], inverse[...])
    sums = jnp.sum(right * right, axis=0, keepdims=True)
    squares[...] = sums
    sent[...] = right / level(sums, right.shape[0])


def normalised(right0, inverse):
    quarter = right0.shape[0]
    return call(
        normal_kernel,
        [shape((quarter, RANK)), shape((1, RANK))],
        [VMEM, VMEM],
        [],
        12 * quarter * RANK * RANK,
        8 * quarter * RANK,
    )(right0, inverse)


def update_kernel(place, momentum, gradient, weight, basis, scale, *refs):
    parts, squares = refs[:NY], refs[NY : 2 * NY]
    new_momentum, new_factor, new_weight, factor, spread = refs[2 * NY :]
    rows, wide = momentum.shape
    step = pl.program_id(0)
    quarter = parts[0].shape[0]

    @pl.when(step == 0)
    def _():
        s = scale[...]
        for k in range(NY):
            row = pl.multiple_of(lax.rem(place[1] + k, NY) * quarter, 64)
            factor[pl.ds(row, quarter), :] = (parts[k][...] * (level(squares[k][:1], quarter) / s)).astype(bf16)
        b = basis[...]
        for i, v in enumerate((b * s, b)):
            hi = v.astype(bf16)
            spread[2 * i * rows : (2 * i + 1) * rows, :] = hi
            spread[(2 * i + 1) * rows : (2 * i + 2) * rows, :] = (v - hi.astype(f32)).astype(bf16)

    f = factor[pl.ds(pl.multiple_of(step * wide, wide), wide), :]
    new_factor[...] = f
    products = lax.dot_general(spread[...], f, (((1,), (1,)), ((), ())), preferred_element_type=f32)

    def times(i):
        return products[2 * i * rows : (2 * i + 1) * rows] + products[(2 * i + 1) * rows : (2 * i + 2) * rows]

    combined = momentum[...] + gradient[...].astype(f32)
    new_momentum[...] = combined - (1.0 - decay_rate) * times(0)
    step_size = learn_rate * (D / RANK) ** 0.5
    new_weight[...] = (weight[...].astype(f32) - step_size * times(1)).astype(bf16)


def update(place, momentum, gradient, weight, basis, scale, parts, squares):
    rows, cols = momentum.shape
    block = pl.BlockSpec((rows, WIDE), lambda i: (0, i))
    whole = lambda a: pl.BlockSpec(a.shape, lambda i: (0, 0))
    return pl.pallas_call(
        update_kernel,
        grid=(cols // WIDE,),
        out_shape=[shape((rows, cols)), shape((cols, RANK), bf16), shape((rows, cols), bf16)],
        in_specs=[SMEM, block, block, block, whole(basis), whole(scale)] + [whole(a) for a in parts + squares],
        out_specs=[block, pl.BlockSpec((WIDE, RANK), lambda i: (i, 0)), block],
        scratch_shapes=[pltpu.VMEM((cols, RANK), bf16), pltpu.VMEM((4 * rows, RANK), bf16)],
        compiler_params=pltpu.CompilerParams(vmem_limit_bytes=40 * 1024 * 1024),
        cost_estimate=pl.CostEstimate(flops=8 * rows * cols * RANK, bytes_accessed=16 * rows * cols, transcendentals=0),
    )(place, momentum, gradient, weight, basis, scale, *parts, *squares)


def over_z(a):
    return lax.all_to_all(a, "dp", 0, 0, axis_index_groups=Z_GROUPS, tiled=True)


def shards(momentum, gradient, factor, weight):
    dp, tp = lax.axis_index("dp"), lax.axis_index("tensor")
    place = jnp.stack([tp % 2, dp // NZ, dp % NZ]).astype(jnp.int32)
    rows, cols = momentum.shape

    flipped, given, kept = project(place, momentum, gradient, factor)
    blocks = lax.all_to_all(flipped, "dp", 0, 0, axis_index_groups=Y_GROUPS, tiled=True)
    pair = kept + lax.ppermute(given, "tensor", OTHER_CORE)
    xs = [pair] + [lax.ppermute(pair, "tensor", from_x(k)) for k in range(1, NX)]
    mine = (xs[0] + xs[2]) + (xs[1] + xs[3])
    mine = [mine] + [lax.ppermute(mine, "dp", from_y(k)) for k in range(1, NY)]

    gram_given, gram_kept, stacked = gram_halves(place, mine, blocks)
    gram_pair = gram_kept + lax.ppermute(gram_given, "tensor", OTHER_CORE)
    other = lax.ppermute(stacked, "tensor", OTHER_CORE)

    right_kept, right_a, right_b, projected = right_sums(place, stacked, other, blocks)
    right_a = lax.ppermute(right_a, "dp", to_neighbour(0))
    right_b = lax.ppermute(right_b, "dp", to_neighbour(1))
    gram_shares = share(over_z(gram_pair))
    gram_shares, right_a, right_b = lax.optimization_barrier((gram_shares, right_a, right_b))
    pairs = shifted(place, right_kept, right_a, right_b)
    pairs = [pairs[0]] + [lax.ppermute(pairs[k], "dp", from_z(NZ - 2 * k)) for k in range(1, NZ // 2)]
    gram_half = over_z(gram_shares)
    gram_other = lax.ppermute(gram_half, "tensor", OTHER_CORE)
    right0 = spread_sum(pairs)
    inverse = inverse_cholesky(place, gram_half, gram_other, right0)
    right0 = over_z(right0)

    basis = dot_t(projected, inverse)
    basis, right0 = lax.optimization_barrier((basis, right0))
    sent, squares = normalised(right0, inverse)
    sent = sent.astype(jnp.float16)
    sent_y = [sent] + [lax.ppermute(sent, "dp", from_y(k)) for k in range(1, NY)]
    squares_x = [squares] + [lax.ppermute(squares, "tensor", from_x(k)) for k in range(1, NX)]
    total = (squares_x[0] + squares_x[2]) + (squares_x[1] + squares_x[3])
    total = total + lax.ppermute(total, "tensor", OTHER_CORE)
    both = jnp.concatenate([squares, total], 0)
    both_y = [both] + [lax.ppermute(both, "dp", from_y(k)) for k in range(1, NY)]
    both_y, sent_y = lax.optimization_barrier((both_y, sent_y))
    total = (both_y[0][1:] + both_y[2][1:]) + (both_y[1][1:] + both_y[3][1:])
    scale = jnp.sqrt(total / (cols * 2 * NX) + epsilon)
    sent_y = [a.astype(f32) for a in sent_y]
    return update(place, momentum, gradient, weight, basis, scale, sent_y, both_y)


def solution(mesh):
    in_specs = (P("dp", "tensor"), P("dp", "tensor"), P("tensor", None), P("dp", "tensor"))
    out_specs = (P("dp", "tensor"), P("tensor", None), P("dp", "tensor"))
    return jax.shard_map(shards, mesh=mesh, in_specs=in_specs, out_specs=out_specs, check_vma=False)
```

```python
import functools

import jax
import jax.numpy as jnp
from jax import lax
from jax.experimental import pallas as pl
from jax.experimental.pallas import tpu as pltpu
from jax.sharding import PartitionSpec as P

D = 8192
RANK = 512
BLOCK = 128
BLOCKS = RANK // BLOCK
UPPER = [(i, j) for i in range(BLOCKS) for j in range(i, BLOCKS)]
NY, NZ, NX = 4, 8, 4

precise = lax.Precision.HIGHEST
decay_rate = 0.95
learn_rate = 0.5
epsilon = 1e-06
f32 = jnp.float32
bf16 = jnp.bfloat16

WIDE = 896
VMEM_LIMIT = 20 * 1024 * 1024
VMEM_ALL = 60 * 1024 * 1024

Y_GROUPS = [[y * NZ + z for y in range(NY)] for z in range(NZ)]
Z_GROUPS = [[y * NZ + z for z in range(NZ)] for y in range(NY)]


def from_y(k):
    return [((i + NZ * k) % (NY * NZ), i) for i in range(NY * NZ)]


def from_z(k):
    return [(i // NZ * NZ + (i + k) % NZ, i) for i in range(NY * NZ)]


def from_x(k):
    return [((i + 2 * k) % (2 * NX), i) for i in range(2 * NX)]


def to_neighbour(odd):
    return [(i, i // NZ * NZ + ((i % NZ + odd ^ 1) - odd) % NZ) for i in range(NY * NZ)]


OTHER_CORE = [(i ^ 1, i) for i in range(2 * NX)]


def sublane(v, i):
    return jnp.broadcast_to(v[i : i + 1, :], (8, BLOCK))


def column(v, c):
    return jnp.broadcast_to(v[:, c : c + 1], (8, BLOCK))


def invert_factor(a):
    lane = lax.broadcasted_iota(jnp.int32, (8, BLOCK), 1)
    sub = lax.broadcasted_iota(jnp.int32, (8, BLOCK), 0)
    out = []
    for p in range(16):
        r = a[p]
        here = (lane >= 8 * p) & (lane < 8 * p + 8)
        cols = [column(r, 8 * p + k) for k in range(8)]
        r = jnp.where(here, jnp.where(lane == sub + 8 * p, 1.0, 0.0), r)
        x = jnp.zeros((8, BLOCK), f32)
        for j in range(8):
            pivot_col = cols[j]
            pivot = sublane(pivot_col, j)
            recip = 1.0 / pivot
            at = sub == j

            def eliminate(v, pivot_col=pivot_col, recip=recip, at=at, j=j):
                row = sublane(v, j) * recip
                return jnp.where(at, row, v - pivot_col * row)

            for k in range(j + 1, 8):
                cols[k] = eliminate(cols[k])
            x = jnp.where(at, sublane(r, j) * lax.rsqrt(pivot), x)
            r = eliminate(r)
        out.append(jnp.where(lane <= sub + 8 * p, x, 0.0))
        rows = [sublane(r, j) for j in range(8)]
        for q in range(p + 1, 16):
            v = a[q]
            t = [column(v, 8 * p + j) * rows[j] for j in range(8)]
            total = ((t[0] + t[1]) + (t[2] + t[3])) + ((t[4] + t[5]) + (t[6] + t[7]))
            a[q] = jnp.where(here, 0.0, v) - total
    return out


def cholesky_kernel(mine_ref, other_ref, after, x_ref, z_ref, g_ref, t_ref):
    few = mine_ref.shape[0]
    core = core_index()
    g_ref[pl.ds(pl.multiple_of(core * few, few), few), :] = mine_ref[...]
    g_ref[pl.ds(pl.multiple_of((1 - core) * few, few), few), :] = other_ref[...]
    for n, (i, j) in enumerate(UPPER):
        z_ref[i * BLOCK : (i + 1) * BLOCK, j * BLOCK : (j + 1) * BLOCK] = g_ref[n * BLOCK : (n + 1) * BLOCK, :]

    def spread_block(b):
        start, end = b * BLOCK, (b + 1) * BLOCK
        t = t_ref[...]
        x_ref[start:end, start:end] = t
        if b > 0:
            x_ref[start:end, :start] = dot(t, z_ref[start:end, :start])
        if b < BLOCKS - 1:
            x_ref[start:end, end:] = jnp.zeros((BLOCK, RANK - end), f32)
            u = dot(t, z_ref[start:end, end:])
            lower = dot_0(u, x_ref[start:end, :end])
            if b > 0:
                z_ref[end:, :start] = z_ref[end:, :start] - lower[:, :start]
            z_ref[end:, start:end] = -lower[:, start:]
            for i in range(b + 1, BLOCKS):
                rows = slice(i * BLOCK, (i + 1) * BLOCK)
                own = u[:, i * BLOCK - end : (i + 1) * BLOCK - end]
                z_ref[rows, i * BLOCK :] = z_ref[rows, i * BLOCK :] - dot_0(own, u[:, i * BLOCK - end :])

    def step(b, carry):
        start = pl.multiple_of(b * BLOCK, BLOCK)
        a = [z_ref[pl.ds(pl.multiple_of(start + 8 * i, 8), 8), pl.ds(start, BLOCK)] for i in range(16)]
        for i, v in enumerate(invert_factor(a)):
            t_ref[8 * i : 8 * i + 8, :] = v
        for c in range(BLOCKS):
            pl.when(b == c)(functools.partial(spread_block, c))
        return carry

    lax.fori_loop(0, BLOCKS, step, 0)


def inverse_cholesky(mine, other, after):
    return call(
        cholesky_kernel,
        [shape((RANK, RANK))],
        [VMEM, VMEM, pl.BlockSpec(memory_space=pl.ANY)],
        [
            pltpu.VMEM((RANK, RANK), f32),
            pltpu.VMEM((len(UPPER) * BLOCK, BLOCK), f32),
            pltpu.VMEM((BLOCK, BLOCK), f32),
        ],
        80 * RANK**3,
        8 * RANK**2,
    )(mine, other, after)[0]


VMEM = pl.BlockSpec(memory_space=pltpu.VMEM)


def core_index():
    return lax.rem(lax.axis_index("tensor"), 2)


def y_index():
    return lax.axis_index("dp") // NZ


def z_index():
    return lax.rem(lax.axis_index("dp"), NZ)


def shape(dims, dtype=f32):
    return jax.ShapeDtypeStruct(dims, dtype)


def dot(a, b):
    return jnp.dot(a, b, precision=precise, preferred_element_type=f32)


def dot_t(a, b):
    return lax.dot_general(a, b, (((1,), (1,)), ((), ())), precision=precise, preferred_element_type=f32)


def dot_0(a, b):
    return lax.dot_general(a, b, (((0,), (0,)), ((), ())), precision=precise, preferred_element_type=f32)


def split3(a):
    hi = a.astype(bf16)
    rest = a - hi.astype(f32)
    mid = rest.astype(bf16)
    return hi, mid, (rest - mid.astype(f32)).astype(bf16)


def call(kernel, outs, ins, scratch, flops, moved):
    return pl.pallas_call(
        kernel,
        out_shape=outs,
        in_specs=ins,
        out_specs=[VMEM] * len(outs),
        scratch_shapes=scratch,
        compiler_params=pltpu.CompilerParams(vmem_limit_bytes=VMEM_LIMIT),
        cost_estimate=pl.CostEstimate(flops=flops, bytes_accessed=moved, transcendentals=0),
    )


def project_kernel(momentum, gradient, factor, flipped, given, kept, total, stacked):
    step, steps = pl.program_id(0), pl.num_programs(0)
    rows, half = momentum.shape[0], given.shape[0]
    combined = momentum[...] + gradient[...].astype(f32)
    flipped[...] = combined.T
    for i, v in enumerate(split3(combined)):
        stacked[i * rows : (i + 1) * rows, :] = v
    parts = jnp.dot(stacked[...], factor[...], preferred_element_type=f32)
    part = (parts[2 * rows :] + parts[rows : 2 * rows]) + parts[:rows]

    @pl.when(step == 0)
    def _():
        total[...] = part

    @pl.when(step > 0)
    def _():
        total[...] += part

    @pl.when(step == steps - 1)
    def _():
        core = core_index()
        given[...] = total[pl.ds(pl.multiple_of((1 - core) * half, half), half), :]
        kept[...] = total[pl.ds(pl.multiple_of(core * half, half), half), :]


def project(momentum, gradient, factor):
    rows, cols = momentum.shape
    half = shape((rows // 2, RANK))
    block = pl.BlockSpec((rows, WIDE), lambda i: (0, i))
    whole = pl.BlockSpec(half.shape, lambda i: (0, 0))
    return pl.pallas_call(
        project_kernel,
        grid=(cols // WIDE,),
        out_shape=[shape((cols, rows)), half, half],
        in_specs=[block, block, pl.BlockSpec((WIDE, RANK), lambda i: (i, 0))],
        out_specs=[pl.BlockSpec((WIDE, rows), lambda i: (i, 0)), whole, whole],
        scratch_shapes=[pltpu.VMEM((rows, RANK), f32), pltpu.VMEM((3 * rows, WIDE), bf16)],
        compiler_params=pltpu.CompilerParams(vmem_limit_bytes=VMEM_ALL),
        cost_estimate=pl.CostEstimate(flops=6 * rows * cols * RANK, bytes_accessed=10 * rows * cols, transcendentals=0),
    )(momentum, gradient, factor)


def gram_kernel(*refs):
    parts, (given, kept, stacked, packed) = refs[:NY], refs[NY:]
    half, few = parts[0].shape[0], given.shape[0]
    for k in range(NY):
        stacked[k * half : (k + 1) * half, :] = parts[k][...]
    n = 0
    for i in range(BLOCKS):
        strip = dot_0(stacked[:, i * BLOCK : (i + 1) * BLOCK], stacked[:, i * BLOCK :])
        for j in range(BLOCKS - i):
            packed[n * BLOCK : (n + 1) * BLOCK, :] = strip[:, j * BLOCK : (j + 1) * BLOCK]
            n += 1
    core = core_index()
    given[...] = packed[pl.ds(pl.multiple_of((1 - core) * few, few), few), :]
    kept[...] = packed[pl.ds(pl.multiple_of(core * few, few), few), :]


def gram_halves(parts):
    few = len(UPPER) * BLOCK // 2
    half = parts[0].shape[0]
    return call(
        gram_kernel,
        [shape((few, BLOCK))] * 2 + [shape((NY * half, RANK))],
        [VMEM] * NY,
        [pltpu.VMEM((2 * few, BLOCK), f32)],
        12 * NY * half * RANK * RANK,
        4 * NY * half * RANK + 8 * few * BLOCK,
    )(*parts)


def share_kernel(swapped, out):
    rows = swapped.shape[0] // NZ
    terms = [swapped[k * rows : (k + 1) * rows, :] for k in range(NZ)]
    total = ((terms[0] + terms[1]) + (terms[2] + terms[3])) + ((terms[4] + terms[5]) + (terms[6] + terms[7]))
    for k in range(NZ):
        out[k * rows : (k + 1) * rows, :] = total


def share(swapped):
    return call(share_kernel, [shape(swapped.shape)], [VMEM], [], 0, 8 * swapped.size)(swapped)[0]


def right_kernel(mine, other, blocks, kept, given_a, given_b, projected, rows_all, cols_all, result):
    half = mine.shape[0] // NY
    eighth = result.shape[1]
    quarter = NZ * eighth
    core, odd = core_index(), lax.rem(z_index(), 2)
    for k in range(NY):
        low = pl.multiple_of(2 * k * half + core * half, half)
        high = pl.multiple_of(2 * k * half + (1 - core) * half, half)
        rows_all[pl.ds(low, half), :] = mine[k * half : (k + 1) * half, :]
        rows_all[pl.ds(high, half), :] = other[k * half : (k + 1) * half, :]
        row = pl.multiple_of(lax.rem(y_index() + k, NY) * quarter, 8)
        cols_all[:, 2 * k * half : 2 * (k + 1) * half] = blocks[pl.ds(row, quarter), :]
    projected[...] = rows_all[: 2 * half, :]
    total = jnp.dot(cols_all[...], rows_all[...], precision=precise, preferred_element_type=f32)
    for s in range(NZ):
        result[s] = total[s * eighth : (s + 1) * eighth, :]
    for s in range(NZ // 2):
        kept[s] = result[2 * s + odd]
        given_a[s] = result[2 * s + 1 - odd, :, : RANK // 2]
        given_b[s] = result[2 * s + 1 - odd, :, RANK // 2 :]


def right_sums(mine, other, blocks):
    cols, rows = blocks.shape
    quarter = cols // NY
    eighth = quarter // NZ
    return call(
        right_kernel,
        [shape((NZ // 2, eighth, RANK))] + [shape((NZ // 2, eighth, RANK // 2))] * 2 + [shape((rows, RANK))],
        [VMEM] * 3,
        [pltpu.VMEM((NY * rows, RANK), f32), pltpu.VMEM((quarter, NY * rows), f32), pltpu.VMEM((NZ, eighth, RANK), f32)],
        12 * quarter * NY * rows * RANK,
        4 * (quarter * NY * rows + NY * rows * RANK + quarter * RANK),
    )(mine, other, blocks)


def shift_kernel(kept, from_a, from_b, *outs):
    for k in range(NZ // 2):
        s = lax.rem(z_index() + 2 * k, NZ) // 2
        outs[k][:, : RANK // 2] = kept[s, :, : RANK // 2] + from_a[s]
        outs[k][:, RANK // 2 :] = kept[s, :, RANK // 2 :] + from_b[s]


def shifted(kept, from_a, from_b):
    eighth = kept.shape[1]
    return call(
        shift_kernel, [shape((eighth, RANK))] * (NZ // 2), [VMEM] * 3, [], 0, 8 * kept.size
    )(kept, from_a, from_b)


def spread_kernel(a, b, c, d, out):
    total = (a[...] + c[...]) + (b[...] + d[...])
    rows = total.shape[0]
    for k in range(NZ):
        out[k * rows : (k + 1) * rows, :] = total


def spread_sum(parts):
    rows, cols = parts[0].shape
    return call(spread_kernel, [shape((NZ * rows, cols))], [VMEM] * len(parts), [], 0, 8 * NZ * rows * cols)(*parts)[0]


def level(squares, count):
    return jnp.sqrt(jnp.maximum(squares / count, 1e-30))


def normal_kernel(right0, inverse, sent, squares):
    right = dot_t(right0[...], inverse[...])
    sums = jnp.sum(right * right, axis=0, keepdims=True)
    squares[...] = sums
    sent[...] = right / level(sums, right.shape[0])


def normalised(right0, inverse):
    quarter = right0.shape[0]
    return call(
        normal_kernel,
        [shape((quarter, RANK)), shape((1, RANK))],
        [VMEM, VMEM],
        [],
        12 * quarter * RANK * RANK,
        8 * quarter * RANK,
    )(right0, inverse)


def update_kernel(momentum, gradient, weight, basis, scale, *refs):
    parts, squares = refs[:NY], refs[NY : 2 * NY]
    new_momentum, new_factor, new_weight, factor, spread = refs[2 * NY :]
    rows, wide = momentum.shape
    step = pl.program_id(0)
    quarter = parts[0].shape[0]

    @pl.when(step == 0)
    def _():
        s = scale[...]
        for k in range(NY):
            row = pl.multiple_of(lax.rem(y_index() + k, NY) * quarter, 64)
            factor[pl.ds(row, quarter), :] = (parts[k][...] * (level(squares[k][:1], quarter) / s)).astype(bf16)
        b = basis[...]
        for i, v in enumerate((b * s, b)):
            hi = v.astype(bf16)
            spread[2 * i * rows : (2 * i + 1) * rows, :] = hi
            spread[(2 * i + 1) * rows : (2 * i + 2) * rows, :] = (v - hi.astype(f32)).astype(bf16)

    f = factor[pl.ds(pl.multiple_of(step * wide, wide), wide), :]
    new_factor[...] = f
    products = lax.dot_general(spread[...], f, (((1,), (1,)), ((), ())), preferred_element_type=f32)

    def times(i):
        return products[2 * i * rows : (2 * i + 1) * rows] + products[(2 * i + 1) * rows : (2 * i + 2) * rows]

    combined = momentum[...] + gradient[...].astype(f32)
    new_momentum[...] = combined - (1.0 - decay_rate) * times(0)
    step_size = learn_rate * (D / RANK) ** 0.5
    new_weight[...] = (weight[...].astype(f32) - step_size * times(1)).astype(bf16)


def update(momentum, gradient, weight, basis, scale, parts, squares):
    rows, cols = momentum.shape
    block = pl.BlockSpec((rows, WIDE), lambda i: (0, i))
    whole = lambda a: pl.BlockSpec(a.shape, lambda i: (0, 0))
    return pl.pallas_call(
        update_kernel,
        grid=(cols // WIDE,),
        out_shape=[shape((rows, cols)), shape((cols, RANK), bf16), shape((rows, cols), bf16)],
        in_specs=[block, block, block, whole(basis), whole(scale)] + [whole(a) for a in parts + squares],
        out_specs=[block, pl.BlockSpec((WIDE, RANK), lambda i: (i, 0)), block],
        scratch_shapes=[pltpu.VMEM((cols, RANK), bf16), pltpu.VMEM((4 * rows, RANK), bf16)],
        compiler_params=pltpu.CompilerParams(vmem_limit_bytes=40 * 1024 * 1024),
        cost_estimate=pl.CostEstimate(flops=8 * rows * cols * RANK, bytes_accessed=16 * rows * cols, transcendentals=0),
    )(momentum, gradient, weight, basis, scale, *parts, *squares)


def over_z(a):
    return lax.all_to_all(a, "dp", 0, 0, axis_index_groups=Z_GROUPS, tiled=True)


def shards(momentum, gradient, factor, weight):
    rows, cols = momentum.shape

    flipped, given, kept = project(momentum, gradient, factor)
    blocks = lax.all_to_all(flipped, "dp", 0, 0, axis_index_groups=Y_GROUPS, tiled=True)
    pair = kept + lax.ppermute(given, "tensor", OTHER_CORE)
    xs = [pair] + [lax.ppermute(pair, "tensor", from_x(k)) for k in range(1, NX)]
    mine = (xs[0] + xs[2]) + (xs[1] + xs[3])
    mine = [mine] + [lax.ppermute(mine, "dp", from_y(k)) for k in range(1, NY)]
    mine, blocks = lax.optimization_barrier((mine, blocks))

    gram_given, gram_kept, stacked = gram_halves(mine)
    gram_pair = gram_kept + lax.ppermute(gram_given, "tensor", OTHER_CORE)
    other = lax.ppermute(stacked, "tensor", OTHER_CORE)

    right_kept, right_a, right_b, projected = right_sums(stacked, other, blocks)
    right_a = lax.ppermute(right_a, "dp", to_neighbour(0))
    right_b = lax.ppermute(right_b, "dp", to_neighbour(1))
    gram_shares = share(over_z(gram_pair))
    gram_shares, right_a, right_b = lax.optimization_barrier((gram_shares, right_a, right_b))
    pairs = shifted(right_kept, right_a, right_b)
    pairs = [pairs[0]] + [lax.ppermute(pairs[k], "dp", from_z(NZ - 2 * k)) for k in range(1, NZ // 2)]
    gram_half = over_z(gram_shares)
    gram_other = lax.ppermute(gram_half, "tensor", OTHER_CORE)
    right0 = spread_sum(pairs)
    inverse = inverse_cholesky(gram_half, gram_other, right0)
    right0 = over_z(right0)

    basis = dot_t(projected, inverse)
    basis, right0 = lax.optimization_barrier((basis, right0))
    sent, squares = normalised(right0, inverse)
    sent = sent.astype(jnp.float16)
    sent_y = [sent] + [lax.ppermute(sent, "dp", from_y(k)) for k in range(1, NY)]
    squares_x = [squares] + [lax.ppermute(squares, "tensor", from_x(k)) for k in range(1, NX)]
    total = (squares_x[0] + squares_x[2]) + (squares_x[1] + squares_x[3])
    total = total + lax.ppermute(total, "tensor", OTHER_CORE)
    both = jnp.concatenate([squares, total], 0)
    both_y = [both] + [lax.ppermute(both, "dp", from_y(k)) for k in range(1, NY)]
    both_y, sent_y = lax.optimization_barrier((both_y, sent_y))
    total = (both_y[0][1:] + both_y[2][1:]) + (both_y[1][1:] + both_y[3][1:])
    scale = jnp.sqrt(total / (cols * 2 * NX) + epsilon)
    sent_y = [a.astype(f32) for a in sent_y]
    return update(momentum, gradient, weight, basis, scale, sent_y, both_y)


def solution(mesh):
    in_specs = (P("dp", "tensor"), P("dp", "tensor"), P("tensor", None), P("dp", "tensor"))
    out_specs = (P("dp", "tensor"), P("tensor", None), P("dp", "tensor"))
    return jax.shard_map(shards, mesh=mesh, in_specs=in_specs, out_specs=out_specs, check_vma=False)
```

```python
import functools

import jax
import jax.numpy as jnp
from jax import lax
from jax.experimental import pallas as pl
from jax.experimental.pallas import tpu as pltpu
from jax.sharding import PartitionSpec as P

D = 8192
RANK = 512
BLOCK = 128
BLOCKS = RANK // BLOCK
UPPER = [(i, j) for i in range(BLOCKS) for j in range(i, BLOCKS)]
NY, NZ, NX = 4, 8, 4

precise = lax.Precision.HIGHEST
decay_rate = 0.95
learn_rate = 0.5
epsilon = 1e-06
f32 = jnp.float32
bf16 = jnp.bfloat16

WIDE = 896
VMEM_LIMIT = 20 * 1024 * 1024
VMEM_ALL = 60 * 1024 * 1024

Y_GROUPS = [[y * NZ + z for y in range(NY)] for z in range(NZ)]
Z_GROUPS = [[y * NZ + z for z in range(NZ)] for y in range(NY)]


def from_y(k):
    return [((i + NZ * k) % (NY * NZ), i) for i in range(NY * NZ)]


def from_z(k):
    return [(i // NZ * NZ + (i + k) % NZ, i) for i in range(NY * NZ)]


def from_x(k):
    return [((i + 2 * k) % (2 * NX), i) for i in range(2 * NX)]


def to_neighbour(odd):
    return [(i, i // NZ * NZ + ((i % NZ + odd ^ 1) - odd) % NZ) for i in range(NY * NZ)]


OTHER_CORE = [(i ^ 1, i) for i in range(2 * NX)]


def sublane(v, i):
    return jnp.broadcast_to(v[i : i + 1, :], (8, BLOCK))


def column(v, c):
    return jnp.broadcast_to(v[:, c : c + 1], (8, BLOCK))


def invert_factor(a):
    lane = lax.broadcasted_iota(jnp.int32, (8, BLOCK), 1)
    sub = lax.broadcasted_iota(jnp.int32, (8, BLOCK), 0)
    out = []
    for p in range(16):
        r = a[p]
        here = (lane >= 8 * p) & (lane < 8 * p + 8)
        cols = [column(r, 8 * p + k) for k in range(8)]
        r = jnp.where(here, jnp.where(lane == sub + 8 * p, 1.0, 0.0), r)
        x = jnp.zeros((8, BLOCK), f32)
        for j in range(8):
            pivot_col = cols[j]
            pivot = sublane(pivot_col, j)
            recip = 1.0 / pivot
            at = sub == j

            def eliminate(v, pivot_col=pivot_col, recip=recip, at=at, j=j):
                row = sublane(v, j) * recip
                return jnp.where(at, row, v - pivot_col * row)

            for k in range(j + 1, 8):
                cols[k] = eliminate(cols[k])
            x = jnp.where(at, sublane(r, j) * lax.rsqrt(pivot), x)
            r = eliminate(r)
        out.append(jnp.where(lane <= sub + 8 * p, x, 0.0))
        rows = [sublane(r, j) for j in range(8)]
        for q in range(p + 1, 16):
            v = a[q]
            t = [column(v, 8 * p + j) * rows[j] for j in range(8)]
            total = ((t[0] + t[1]) + (t[2] + t[3])) + ((t[4] + t[5]) + (t[6] + t[7]))
            a[q] = jnp.where(here, 0.0, v) - total
    return out


def cholesky_kernel(mine_ref, other_ref, after, x_ref, z_ref, g_ref, t_ref):
    few = mine_ref.shape[0]
    core = core_index()
    g_ref[pl.ds(pl.multiple_of(core * few, few), few), :] = mine_ref[...]
    g_ref[pl.ds(pl.multiple_of((1 - core) * few, few), few), :] = other_ref[...]
    for n, (i, j) in enumerate(UPPER):
        z_ref[i * BLOCK : (i + 1) * BLOCK, j * BLOCK : (j + 1) * BLOCK] = g_ref[n * BLOCK : (n + 1) * BLOCK, :]

    def spread_block(b):
        start, end = b * BLOCK, (b + 1) * BLOCK
        t = t_ref[...]
        x_ref[start:end, start:end] = t
        if b > 0:
            x_ref[start:end, :start] = dot(t, z_ref[start:end, :start])
        if b < BLOCKS - 1:
            x_ref[start:end, end:] = jnp.zeros((BLOCK, RANK - end), f32)
            u = dot(t, z_ref[start:end, end:])
            lower = dot_0(u, x_ref[start:end, :end])
            if b > 0:
                z_ref[end:, :start] = z_ref[end:, :start] - lower[:, :start]
            z_ref[end:, start:end] = -lower[:, start:]
            for i in range(b + 1, BLOCKS):
                rows = slice(i * BLOCK, (i + 1) * BLOCK)
                own = u[:, i * BLOCK - end : (i + 1) * BLOCK - end]
                z_ref[rows, i * BLOCK :] = z_ref[rows, i * BLOCK :] - dot_0(own, u[:, i * BLOCK - end :])

    def step(b, carry):
        start = pl.multiple_of(b * BLOCK, BLOCK)
        a = [z_ref[pl.ds(pl.multiple_of(start + 8 * i, 8), 8), pl.ds(start, BLOCK)] for i in range(16)]
        for i, v in enumerate(invert_factor(a)):
            t_ref[8 * i : 8 * i + 8, :] = v
        for c in range(BLOCKS):
            pl.when(b == c)(functools.partial(spread_block, c))
        return carry

    lax.fori_loop(0, BLOCKS, step, 0)


def inverse_cholesky(mine, other, after):
    return call(
        cholesky_kernel,
        [shape((RANK, RANK))],
        [VMEM, VMEM, pl.BlockSpec(memory_space=pl.ANY)],
        [
            pltpu.VMEM((RANK, RANK), f32),
            pltpu.VMEM((len(UPPER) * BLOCK, BLOCK), f32),
            pltpu.VMEM((BLOCK, BLOCK), f32),
        ],
        80 * RANK**3,
        8 * RANK**2,
    )(mine, other, after)[0]


VMEM = pl.BlockSpec(memory_space=pltpu.VMEM)


def core_index():
    return lax.rem(lax.axis_index("tensor"), 2)


def y_index():
    return lax.axis_index("dp") // NZ


def z_index():
    return lax.rem(lax.axis_index("dp"), NZ)


def shape(dims, dtype=f32):
    return jax.ShapeDtypeStruct(dims, dtype)


def dot(a, b):
    return jnp.dot(a, b, precision=precise, preferred_element_type=f32)


def dot_t(a, b):
    return lax.dot_general(a, b, (((1,), (1,)), ((), ())), precision=precise, preferred_element_type=f32)


def dot_0(a, b):
    return lax.dot_general(a, b, (((0,), (0,)), ((), ())), precision=precise, preferred_element_type=f32)


def split3(a):
    hi = a.astype(bf16)
    rest = a - hi.astype(f32)
    mid = rest.astype(bf16)
    return hi, mid, (rest - mid.astype(f32)).astype(bf16)


def call(kernel, outs, ins, scratch, flops, moved):
    return pl.pallas_call(
        kernel,
        out_shape=outs,
        in_specs=ins,
        out_specs=[VMEM] * len(outs),
        scratch_shapes=scratch,
        compiler_params=pltpu.CompilerParams(vmem_limit_bytes=VMEM_LIMIT),
        cost_estimate=pl.CostEstimate(flops=flops, bytes_accessed=moved, transcendentals=0),
    )


def project_kernel(momentum, gradient, factor, flipped, given, kept, total, stacked):
    step, steps = pl.program_id(0), pl.num_programs(0)
    rows, half = momentum.shape[0], given.shape[0]
    combined = momentum[...] + gradient[...].astype(f32)
    flipped[...] = combined.T
    for i, v in enumerate(split3(combined)):
        stacked[i * rows : (i + 1) * rows, :] = v
    parts = jnp.dot(stacked[...], factor[...], preferred_element_type=f32)
    part = (parts[2 * rows :] + parts[rows : 2 * rows]) + parts[:rows]

    @pl.when(step == 0)
    def _():
        total[...] = part

    @pl.when(step > 0)
    def _():
        total[...] += part

    @pl.when(step == steps - 1)
    def _():
        core = core_index()
        given[...] = total[pl.ds(pl.multiple_of((1 - core) * half, half), half), :]
        kept[...] = total[pl.ds(pl.multiple_of(core * half, half), half), :]


def project(momentum, gradient, factor):
    rows, cols = momentum.shape
    half = shape((rows // 2, RANK))
    block = pl.BlockSpec((rows, WIDE), lambda i: (0, i))
    whole = pl.BlockSpec(half.shape, lambda i: (0, 0))
    return pl.pallas_call(
        project_kernel,
        grid=(cols // WIDE,),
        out_shape=[shape((cols, rows)), half, half],
        in_specs=[block, block, pl.BlockSpec((WIDE, RANK), lambda i: (i, 0))],
        out_specs=[pl.BlockSpec((WIDE, rows), lambda i: (i, 0)), whole, whole],
        scratch_shapes=[pltpu.VMEM((rows, RANK), f32), pltpu.VMEM((3 * rows, WIDE), bf16)],
        compiler_params=pltpu.CompilerParams(vmem_limit_bytes=VMEM_ALL),
        cost_estimate=pl.CostEstimate(flops=6 * rows * cols * RANK, bytes_accessed=10 * rows * cols, transcendentals=0),
    )(momentum, gradient, factor)


def gram_kernel(*refs):
    parts, (given, kept, stacked, packed) = refs[:NY], refs[NY:]
    half, few = parts[0].shape[0], given.shape[0]
    for k in range(NY):
        stacked[k * half : (k + 1) * half, :] = parts[k][...]
    n = 0
    for i in range(BLOCKS):
        strip = dot_0(stacked[:, i * BLOCK : (i + 1) * BLOCK], stacked[:, i * BLOCK :])
        for j in range(BLOCKS - i):
            packed[n * BLOCK : (n + 1) * BLOCK, :] = strip[:, j * BLOCK : (j + 1) * BLOCK]
            n += 1
    core = core_index()
    given[...] = packed[pl.ds(pl.multiple_of((1 - core) * few, few), few), :]
    kept[...] = packed[pl.ds(pl.multiple_of(core * few, few), few), :]


def gram_halves(parts):
    few = len(UPPER) * BLOCK // 2
    half = parts[0].shape[0]
    return call(
        gram_kernel,
        [shape((few, BLOCK))] * 2 + [shape((NY * half, RANK))],
        [VMEM] * NY,
        [pltpu.VMEM((2 * few, BLOCK), f32)],
        12 * NY * half * RANK * RANK,
        4 * NY * half * RANK + 8 * few * BLOCK,
    )(*parts)


def share_kernel(swapped, out):
    rows = swapped.shape[0] // NZ
    terms = [swapped[k * rows : (k + 1) * rows, :] for k in range(NZ)]
    total = ((terms[0] + terms[1]) + (terms[2] + terms[3])) + ((terms[4] + terms[5]) + (terms[6] + terms[7]))
    for k in range(NZ):
        out[k * rows : (k + 1) * rows, :] = total


def share(swapped):
    return call(share_kernel, [shape(swapped.shape)], [VMEM], [], 0, 8 * swapped.size)(swapped)[0]


def right_kernel(mine, other, blocks, kept, given_a, given_b, projected, rows_all, cols_all, result):
    half = mine.shape[0] // NY
    eighth = result.shape[1]
    quarter = NZ * eighth
    core, odd = core_index(), lax.rem(z_index(), 2)
    for k in range(NY):
        low = pl.multiple_of(2 * k * half + core * half, half)
        high = pl.multiple_of(2 * k * half + (1 - core) * half, half)
        rows_all[pl.ds(low, half), :] = mine[k * half : (k + 1) * half, :]
        rows_all[pl.ds(high, half), :] = other[k * half : (k + 1) * half, :]
        row = pl.multiple_of(lax.rem(y_index() + k, NY) * quarter, 8)
        cols_all[:, 2 * k * half : 2 * (k + 1) * half] = blocks[pl.ds(row, quarter), :]
    projected[...] = rows_all[: 2 * half, :]
    total = jnp.dot(cols_all[...], rows_all[...], precision=precise, preferred_element_type=f32)
    for s in range(NZ):
        result[s] = total[s * eighth : (s + 1) * eighth, :]
    for s in range(NZ // 2):
        kept[s] = result[2 * s + odd]
        given_a[s] = result[2 * s + 1 - odd, :, : RANK // 2]
        given_b[s] = result[2 * s + 1 - odd, :, RANK // 2 :]


def right_sums(mine, other, blocks):
    cols, rows = blocks.shape
    quarter = cols // NY
    eighth = quarter // NZ
    return call(
        right_kernel,
        [shape((NZ // 2, eighth, RANK))] + [shape((NZ // 2, eighth, RANK // 2))] * 2 + [shape((rows, RANK))],
        [VMEM] * 3,
        [pltpu.VMEM((NY * rows, RANK), f32), pltpu.VMEM((quarter, NY * rows), f32), pltpu.VMEM((NZ, eighth, RANK), f32)],
        12 * quarter * NY * rows * RANK,
        4 * (quarter * NY * rows + NY * rows * RANK + quarter * RANK),
    )(mine, other, blocks)


def shift_kernel(kept, from_a, from_b, *outs):
    for k in range(NZ // 2):
        s = lax.rem(z_index() + 2 * k, NZ) // 2
        outs[k][:, : RANK // 2] = kept[s, :, : RANK // 2] + from_a[s]
        outs[k][:, RANK // 2 :] = kept[s, :, RANK // 2 :] + from_b[s]


def shifted(kept, from_a, from_b):
    eighth = kept.shape[1]
    return call(
        shift_kernel, [shape((eighth, RANK))] * (NZ // 2), [VMEM] * 3, [], 0, 8 * kept.size
    )(kept, from_a, from_b)


def spread_kernel(a, b, c, d, out):
    total = (a[...] + c[...]) + (b[...] + d[...])
    rows = total.shape[0]
    for k in range(NZ):
        out[k * rows : (k + 1) * rows, :] = total


def spread_sum(parts):
    rows, cols = parts[0].shape
    return call(spread_kernel, [shape((NZ * rows, cols))], [VMEM] * len(parts), [], 0, 8 * NZ * rows * cols)(*parts)[0]


def level(squares, count):
    return jnp.sqrt(jnp.maximum(squares / count, 1e-30))


def normal_kernel(right0, inverse, sent, squares):
    right = dot_t(right0[...], inverse[...])
    sums = jnp.sum(right * right, axis=0, keepdims=True)
    squares[...] = sums
    sent[...] = right / level(sums, right.shape[0])


def normalised(right0, inverse):
    quarter = right0.shape[0]
    return call(
        normal_kernel,
        [shape((quarter, RANK)), shape((1, RANK))],
        [VMEM, VMEM],
        [],
        12 * quarter * RANK * RANK,
        8 * quarter * RANK,
    )(right0, inverse)


def update_kernel(momentum, gradient, weight, basis, scale, *refs):
    parts, squares = refs[:NY], refs[NY : 2 * NY]
    new_momentum, new_factor, new_weight, factor, spread = refs[2 * NY :]
    rows, wide = momentum.shape
    step = pl.program_id(0)
    quarter = parts[0].shape[0]

    @pl.when(step == 0)
    def _():
        s = scale[...]
        for k in range(NY):
            row = pl.multiple_of(lax.rem(y_index() + k, NY) * quarter, 64)
            factor[pl.ds(row, quarter), :] = (parts[k][...] * (level(squares[k][:1], quarter) / s)).astype(bf16)
        b = basis[...]
        for i, v in enumerate((b * s, b)):
            hi = v.astype(bf16)
            spread[2 * i * rows : (2 * i + 1) * rows, :] = hi
            spread[(2 * i + 1) * rows : (2 * i + 2) * rows, :] = (v - hi.astype(f32)).astype(bf16)

    f = factor[pl.ds(pl.multiple_of(step * wide, wide), wide), :]
    new_factor[...] = f
    products = lax.dot_general(spread[...], f, (((1,), (1,)), ((), ())), preferred_element_type=f32)

    def times(i):
        return products[2 * i * rows : (2 * i + 1) * rows] + products[(2 * i + 1) * rows : (2 * i + 2) * rows]

    combined = momentum[...] + gradient[...].astype(f32)
    new_momentum[...] = combined - (1.0 - decay_rate) * times(0)
    step_size = learn_rate * (D / RANK) ** 0.5
    new_weight[...] = (weight[...].astype(f32) - step_size * times(1)).astype(bf16)


def update(momentum, gradient, weight, basis, scale, parts, squares):
    rows, cols = momentum.shape
    block = pl.BlockSpec((rows, WIDE), lambda i: (0, i))
    whole = lambda a: pl.BlockSpec(a.shape, lambda i: (0, 0))
    return pl.pallas_call(
        update_kernel,
        grid=(cols // WIDE,),
        out_shape=[shape((rows, cols)), shape((cols, RANK), bf16), shape((rows, cols), bf16)],
        in_specs=[block, block, block, whole(basis), whole(scale)] + [whole(a) for a in parts + squares],
        out_specs=[block, pl.BlockSpec((WIDE, RANK), lambda i: (i, 0)), block],
        scratch_shapes=[pltpu.VMEM((cols, RANK), bf16), pltpu.VMEM((4 * rows, RANK), bf16)],
        compiler_params=pltpu.CompilerParams(vmem_limit_bytes=40 * 1024 * 1024),
        cost_estimate=pl.CostEstimate(flops=8 * rows * cols * RANK, bytes_accessed=16 * rows * cols, transcendentals=0),
    )(momentum, gradient, weight, basis, scale, *parts, *squares)


def over_z(a):
    return lax.all_to_all(a, "dp", 0, 0, axis_index_groups=Z_GROUPS, tiled=True)


def shards(momentum, gradient, factor, weight):
    rows, cols = momentum.shape

    flipped, given, kept = project(momentum, gradient, factor)
    blocks = lax.all_to_all(flipped, "dp", 0, 0, axis_index_groups=Y_GROUPS, tiled=True)
    pair = kept + lax.ppermute(given, "tensor", OTHER_CORE)
    xs = [pair] + [lax.ppermute(pair, "tensor", from_x(k)) for k in range(1, NX)]
    mine = (xs[0] + xs[2]) + (xs[1] + xs[3])
    mine = [mine] + [lax.ppermute(mine, "dp", from_y(k)) for k in range(1, NY)]

    gram_given, gram_kept, stacked = gram_halves(mine)
    gram_pair = gram_kept + lax.ppermute(gram_given, "tensor", OTHER_CORE)
    stacked, blocks = lax.optimization_barrier((stacked, blocks))
    other = lax.ppermute(stacked, "tensor", OTHER_CORE)

    right_kept, right_a, right_b, projected = right_sums(stacked, other, blocks)
    right_a = lax.ppermute(right_a, "dp", to_neighbour(0))
    right_b = lax.ppermute(right_b, "dp", to_neighbour(1))
    gram_shares = share(over_z(gram_pair))
    gram_shares, right_a, right_b = lax.optimization_barrier((gram_shares, right_a, right_b))
    pairs = shifted(right_kept, right_a, right_b)
    pairs = [pairs[0]] + [lax.ppermute(pairs[k], "dp", from_z(NZ - 2 * k)) for k in range(1, NZ // 2)]
    gram_half = over_z(gram_shares)
    gram_other = lax.ppermute(gram_half, "tensor", OTHER_CORE)
    right0 = spread_sum(pairs)
    inverse = inverse_cholesky(gram_half, gram_other, right0)
    right0 = over_z(right0)

    basis = dot_t(projected, inverse)
    basis, right0 = lax.optimization_barrier((basis, right0))
    sent, squares = normalised(right0, inverse)
    sent = sent.astype(jnp.float16)
    sent_y = [sent] + [lax.ppermute(sent, "dp", from_y(k)) for k in range(1, NY)]
    squares_x = [squares] + [lax.ppermute(squares, "tensor", from_x(k)) for k in range(1, NX)]
    total = (squares_x[0] + squares_x[2]) + (squares_x[1] + squares_x[3])
    total = total + lax.ppermute(total, "tensor", OTHER_CORE)
    both = jnp.concatenate([squares, total], 0)
    both_y = [both] + [lax.ppermute(both, "dp", from_y(k)) for k in range(1, NY)]
    both_y, sent_y = lax.optimization_barrier((both_y, sent_y))
    total = (both_y[0][1:] + both_y[2][1:]) + (both_y[1][1:] + both_y[3][1:])
    scale = jnp.sqrt(total / (cols * 2 * NX) + epsilon)
    sent_y = [a.astype(f32) for a in sent_y]
    return update(momentum, gradient, weight, basis, scale, sent_y, both_y)


def solution(mesh):
    in_specs = (P("dp", "tensor"), P("dp", "tensor"), P("tensor", None), P("dp", "tensor"))
    out_specs = (P("dp", "tensor"), P("tensor", None), P("dp", "tensor"))
    return jax.shard_map(shards, mesh=mesh, in_specs=in_specs, out_specs=out_specs, check_vma=False)
```

```python
import functools

import jax
import jax.numpy as jnp
from jax import lax
from jax.experimental import pallas as pl
from jax.experimental.pallas import tpu as pltpu
from jax.sharding import PartitionSpec as P

D = 8192
RANK = 512
BLOCK = 128
BLOCKS = RANK // BLOCK
UPPER = [(i, j) for i in range(BLOCKS) for j in range(i, BLOCKS)]
NY, NZ, NX = 4, 8, 4

precise = lax.Precision.HIGHEST
decay_rate = 0.95
learn_rate = 0.5
epsilon = 1e-06
f32 = jnp.float32
bf16 = jnp.bfloat16

WIDE = 896
VMEM_LIMIT = 20 * 1024 * 1024
VMEM_ALL = 60 * 1024 * 1024

Y_GROUPS = [[y * NZ + z for y in range(NY)] for z in range(NZ)]
Z_GROUPS = [[y * NZ + z for z in range(NZ)] for y in range(NY)]


def from_y(k):
    return [((i + NZ * k) % (NY * NZ), i) for i in range(NY * NZ)]


def from_z(k):
    return [(i // NZ * NZ + (i + k) % NZ, i) for i in range(NY * NZ)]


def from_x(k):
    return [((i + 2 * k) % (2 * NX), i) for i in range(2 * NX)]


def to_neighbour(odd):
    return [(i, i // NZ * NZ + ((i % NZ + odd ^ 1) - odd) % NZ) for i in range(NY * NZ)]


OTHER_CORE = [(i ^ 1, i) for i in range(2 * NX)]


def sublane(v, i):
    return jnp.broadcast_to(v[i : i + 1, :], (8, BLOCK))


def column(v, c):
    return jnp.broadcast_to(v[:, c : c + 1], (8, BLOCK))


def invert_factor(a):
    lane = lax.broadcasted_iota(jnp.int32, (8, BLOCK), 1)
    sub = lax.broadcasted_iota(jnp.int32, (8, BLOCK), 0)
    out = []
    for p in range(16):
        r = a[p]
        here = (lane >= 8 * p) & (lane < 8 * p + 8)
        cols = [column(r, 8 * p + k) for k in range(8)]
        r = jnp.where(here, jnp.where(lane == sub + 8 * p, 1.0, 0.0), r)
        x = jnp.zeros((8, BLOCK), f32)
        for j in range(8):
            pivot_col = cols[j]
            pivot = sublane(pivot_col, j)
            recip = 1.0 / pivot
            at = sub == j

            def eliminate(v, pivot_col=pivot_col, recip=recip, at=at, j=j):
                row = sublane(v, j) * recip
                return jnp.where(at, row, v - pivot_col * row)

            for k in range(j + 1, 8):
                cols[k] = eliminate(cols[k])
            x = jnp.where(at, sublane(r, j) * lax.rsqrt(pivot), x)
            r = eliminate(r)
        out.append(jnp.where(lane <= sub + 8 * p, x, 0.0))
        rows = [sublane(r, j) for j in range(8)]
        for q in range(p + 1, 16):
            v = a[q]
            t = [column(v, 8 * p + j) * rows[j] for j in range(8)]
            total = ((t[0] + t[1]) + (t[2] + t[3])) + ((t[4] + t[5]) + (t[6] + t[7]))
            a[q] = jnp.where(here, 0.0, v) - total
    return out


def cholesky_kernel(mine_ref, other_ref, after, x_ref, z_ref, g_ref, t_ref):
    few = mine_ref.shape[0]
    core = core_index()
    g_ref[pl.ds(pl.multiple_of(core * few, few), few), :] = mine_ref[...]
    g_ref[pl.ds(pl.multiple_of((1 - core) * few, few), few), :] = other_ref[...]
    for n, (i, j) in enumerate(UPPER):
        z_ref[i * BLOCK : (i + 1) * BLOCK, j * BLOCK : (j + 1) * BLOCK] = g_ref[n * BLOCK : (n + 1) * BLOCK, :]

    def spread_block(b):
        start, end = b * BLOCK, (b + 1) * BLOCK
        t = t_ref[...]
        x_ref[start:end, start:end] = t
        if b > 0:
            x_ref[start:end, :start] = dot(t, z_ref[start:end, :start])
        if b < BLOCKS - 1:
            x_ref[start:end, end:] = jnp.zeros((BLOCK, RANK - end), f32)
            u = dot(t, z_ref[start:end, end:])
            lower = dot_0(u, x_ref[start:end, :end])
            if b > 0:
                z_ref[end:, :start] = z_ref[end:, :start] - lower[:, :start]
            z_ref[end:, start:end] = -lower[:, start:]
            for i in range(b + 1, BLOCKS):
                rows = slice(i * BLOCK, (i + 1) * BLOCK)
                own = u[:, i * BLOCK - end : (i + 1) * BLOCK - end]
                z_ref[rows, i * BLOCK :] = z_ref[rows, i * BLOCK :] - dot_0(own, u[:, i * BLOCK - end :])

    def step(b, carry):
        start = pl.multiple_of(b * BLOCK, BLOCK)
        a = [z_ref[pl.ds(pl.multiple_of(start + 8 * i, 8), 8), pl.ds(start, BLOCK)] for i in range(16)]
        for i, v in enumerate(invert_factor(a)):
            t_ref[8 * i : 8 * i + 8, :] = v
        for c in range(BLOCKS):
            pl.when(b == c)(functools.partial(spread_block, c))
        return carry

    lax.fori_loop(0, BLOCKS, step, 0)


def inverse_cholesky(mine, other, after):
    return call(
        cholesky_kernel,
        [shape((RANK, RANK))],
        [VMEM, VMEM, pl.BlockSpec(memory_space=pl.ANY)],
        [
            pltpu.VMEM((RANK, RANK), f32),
            pltpu.VMEM((len(UPPER) * BLOCK, BLOCK), f32),
            pltpu.VMEM((BLOCK, BLOCK), f32),
        ],
        80 * RANK**3,
        8 * RANK**2,
    )(mine, other, after)[0]


VMEM = pl.BlockSpec(memory_space=pltpu.VMEM)


def core_index():
    return lax.rem(lax.axis_index("tensor"), 2)


def y_index():
    return lax.axis_index("dp") // NZ


def z_index():
    return lax.rem(lax.axis_index("dp"), NZ)


def shape(dims, dtype=f32):
    return jax.ShapeDtypeStruct(dims, dtype)


def dot(a, b):
    return jnp.dot(a, b, precision=precise, preferred_element_type=f32)


def dot_t(a, b):
    return lax.dot_general(a, b, (((1,), (1,)), ((), ())), precision=precise, preferred_element_type=f32)


def dot_0(a, b):
    return lax.dot_general(a, b, (((0,), (0,)), ((), ())), precision=precise, preferred_element_type=f32)


def split3(a):
    hi = a.astype(bf16)
    rest = a - hi.astype(f32)
    mid = rest.astype(bf16)
    return hi, mid, (rest - mid.astype(f32)).astype(bf16)


def call(kernel, outs, ins, scratch, flops, moved):
    return pl.pallas_call(
        kernel,
        out_shape=outs,
        in_specs=ins,
        out_specs=[VMEM] * len(outs),
        scratch_shapes=scratch,
        compiler_params=pltpu.CompilerParams(vmem_limit_bytes=VMEM_LIMIT),
        cost_estimate=pl.CostEstimate(flops=flops, bytes_accessed=moved, transcendentals=0),
    )


def project_kernel(momentum, gradient, factor, flipped, given, kept, total, stacked):
    step, steps = pl.program_id(0), pl.num_programs(0)
    rows, half = momentum.shape[0], given.shape[0]
    combined = momentum[...] + gradient[...].astype(f32)
    flipped[...] = combined.T
    for i, v in enumerate(split3(combined)):
        stacked[i * rows : (i + 1) * rows, :] = v
    parts = jnp.dot(stacked[...], factor[...], preferred_element_type=f32)
    part = (parts[2 * rows :] + parts[rows : 2 * rows]) + parts[:rows]

    @pl.when(step == 0)
    def _():
        total[...] = part

    @pl.when(step > 0)
    def _():
        total[...] += part

    @pl.when(step == steps - 1)
    def _():
        core = core_index()
        given[...] = total[pl.ds(pl.multiple_of((1 - core) * half, half), half), :]
        kept[...] = total[pl.ds(pl.multiple_of(core * half, half), half), :]


def project(momentum, gradient, factor):
    rows, cols = momentum.shape
    half = shape((rows // 2, RANK))
    block = pl.BlockSpec((rows, WIDE), lambda i: (0, i))
    whole = pl.BlockSpec(half.shape, lambda i: (0, 0))
    return pl.pallas_call(
        project_kernel,
        grid=(cols // WIDE,),
        out_shape=[shape((cols, rows)), half, half],
        in_specs=[block, block, pl.BlockSpec((WIDE, RANK), lambda i: (i, 0))],
        out_specs=[pl.BlockSpec((WIDE, rows), lambda i: (i, 0)), whole, whole],
        scratch_shapes=[pltpu.VMEM((rows, RANK), f32), pltpu.VMEM((3 * rows, WIDE), bf16)],
        compiler_params=pltpu.CompilerParams(vmem_limit_bytes=VMEM_ALL),
        cost_estimate=pl.CostEstimate(flops=6 * rows * cols * RANK, bytes_accessed=10 * rows * cols, transcendentals=0),
    )(momentum, gradient, factor)


def gram_kernel(*refs):
    parts, (given, kept, stacked, packed) = refs[:NY], refs[NY:]
    half, few = parts[0].shape[0], given.shape[0]
    for k in range(NY):
        stacked[k * half : (k + 1) * half, :] = parts[k][...]
    n = 0
    for i in range(BLOCKS):
        strip = dot_0(stacked[:, i * BLOCK : (i + 1) * BLOCK], stacked[:, i * BLOCK :])
        for j in range(BLOCKS - i):
            packed[n * BLOCK : (n + 1) * BLOCK, :] = strip[:, j * BLOCK : (j + 1) * BLOCK]
            n += 1
    core = core_index()
    given[...] = packed[pl.ds(pl.multiple_of((1 - core) * few, few), few), :]
    kept[...] = packed[pl.ds(pl.multiple_of(core * few, few), few), :]


def gram_halves(parts):
    few = len(UPPER) * BLOCK // 2
    half = parts[0].shape[0]
    return call(
        gram_kernel,
        [shape((few, BLOCK))] * 2 + [shape((NY * half, RANK))],
        [VMEM] * NY,
        [pltpu.VMEM((2 * few, BLOCK), f32)],
        12 * NY * half * RANK * RANK,
        4 * NY * half * RANK + 8 * few * BLOCK,
    )(*parts)


def share_kernel(swapped, out):
    rows = swapped.shape[0] // NZ
    terms = [swapped[k * rows : (k + 1) * rows, :] for k in range(NZ)]
    total = ((terms[0] + terms[1]) + (terms[2] + terms[3])) + ((terms[4] + terms[5]) + (terms[6] + terms[7]))
    for k in range(NZ):
        out[k * rows : (k + 1) * rows, :] = total


def share(swapped):
    return call(share_kernel, [shape(swapped.shape)], [VMEM], [], 0, 8 * swapped.size)(swapped)[0]


def right_kernel(mine, other, blocks, kept, given_a, given_b, projected, rows_all, cols_all, result):
    half = mine.shape[0] // NY
    eighth = result.shape[1]
    quarter = NZ * eighth
    core, odd = core_index(), lax.rem(z_index(), 2)
    for k in range(NY):
        low = pl.multiple_of(2 * k * half + core * half, half)
        high = pl.multiple_of(2 * k * half + (1 - core) * half, half)
        rows_all[pl.ds(low, half), :] = mine[k * half : (k + 1) * half, :]
        rows_all[pl.ds(high, half), :] = other[k * half : (k + 1) * half, :]
        row = pl.multiple_of(lax.rem(y_index() + k, NY) * quarter, 8)
        cols_all[:, 2 * k * half : 2 * (k + 1) * half] = blocks[pl.ds(row, quarter), :]
    projected[...] = rows_all[: 2 * half, :]
    total = jnp.dot(cols_all[...], rows_all[...], precision=precise, preferred_element_type=f32)
    for s in range(NZ):
        result[s] = total[s * eighth : (s + 1) * eighth, :]
    for s in range(NZ // 2):
        kept[s] = result[2 * s + odd]
        given_a[s] = result[2 * s + 1 - odd, :, : RANK // 2]
        given_b[s] = result[2 * s + 1 - odd, :, RANK // 2 :]


def right_sums(mine, other, blocks):
    cols, rows = blocks.shape
    quarter = cols // NY
    eighth = quarter // NZ
    return call(
        right_kernel,
        [shape((NZ // 2, eighth, RANK))] + [shape((NZ // 2, eighth, RANK // 2))] * 2 + [shape((rows, RANK))],
        [VMEM] * 3,
        [pltpu.VMEM((NY * rows, RANK), f32), pltpu.VMEM((quarter, NY * rows), f32), pltpu.VMEM((NZ, eighth, RANK), f32)],
        12 * quarter * NY * rows * RANK,
        4 * (quarter * NY * rows + NY * rows * RANK + quarter * RANK),
    )(mine, other, blocks)


def shift_kernel(kept, from_a, from_b, *outs):
    for k in range(NZ // 2):
        s = lax.rem(z_index() + 2 * k, NZ) // 2
        outs[k][:, : RANK // 2] = kept[s, :, : RANK // 2] + from_a[s]
        outs[k][:, RANK // 2 :] = kept[s, :, RANK // 2 :] + from_b[s]


def shifted(kept, from_a, from_b):
    eighth = kept.shape[1]
    return call(
        shift_kernel, [shape((eighth, RANK))] * (NZ // 2), [VMEM] * 3, [], 0, 8 * kept.size
    )(kept, from_a, from_b)


def spread_kernel(a, b, c, d, out):
    total = (a[...] + c[...]) + (b[...] + d[...])
    rows = total.shape[0]
    for k in range(NZ):
        out[k * rows : (k + 1) * rows, :] = total


def spread_sum(parts):
    rows, cols = parts[0].shape
    return call(spread_kernel, [shape((NZ * rows, cols))], [VMEM] * len(parts), [], 0, 8 * NZ * rows * cols)(*parts)[0]


def level(squares, count):
    return jnp.sqrt(jnp.maximum(squares / count, 1e-30))


def normal_kernel(right0, projected, inverse, sent, squares, basis, stacked):
    quarter = right0.shape[0]
    stacked[:quarter, :] = right0[...]
    stacked[quarter:, :] = projected[...]
    both = dot_t(stacked[...], inverse[...])
    right = both[:quarter]
    sums = jnp.sum(right * right, axis=0, keepdims=True)
    squares[...] = sums
    sent[...] = right / level(sums, quarter)
    basis[...] = both[quarter:]


def normalised(right0, projected, inverse):
    quarter, rows = right0.shape[0], projected.shape[0]
    return call(
        normal_kernel,
        [shape((quarter, RANK)), shape((1, RANK)), shape((rows, RANK))],
        [VMEM] * 3,
        [pltpu.VMEM((quarter + rows, RANK), f32)],
        12 * (quarter + rows) * RANK * RANK,
        8 * (quarter + rows) * RANK,
    )(right0, projected, inverse)


def update_kernel(momentum, gradient, weight, basis, scale, *refs):
    parts, squares = refs[:NY], refs[NY : 2 * NY]
    new_momentum, new_factor, new_weight, factor, spread = refs[2 * NY :]
    rows, wide = momentum.shape
    step = pl.program_id(0)
    quarter = parts[0].shape[0]

    @pl.when(step == 0)
    def _():
        s = scale[...]
        for k in range(NY):
            row = pl.multiple_of(lax.rem(y_index() + k, NY) * quarter, 64)
            factor[pl.ds(row, quarter), :] = (parts[k][...] * (level(squares[k][:1], quarter) / s)).astype(bf16)
        b = basis[...]
        for i, v in enumerate((b * s, b)):
            hi = v.astype(bf16)
            spread[2 * i * rows : (2 * i + 1) * rows, :] = hi
            spread[(2 * i + 1) * rows : (2 * i + 2) * rows, :] = (v - hi.astype(f32)).astype(bf16)

    f = factor[pl.ds(pl.multiple_of(step * wide, wide), wide), :]
    new_factor[...] = f
    products = lax.dot_general(spread[...], f, (((1,), (1,)), ((), ())), preferred_element_type=f32)

    def times(i):
        return products[2 * i * rows : (2 * i + 1) * rows] + products[(2 * i + 1) * rows : (2 * i + 2) * rows]

    combined = momentum[...] + gradient[...].astype(f32)
    new_momentum[...] = combined - (1.0 - decay_rate) * times(0)
    step_size = learn_rate * (D / RANK) ** 0.5
    new_weight[...] = (weight[...].astype(f32) - step_size * times(1)).astype(bf16)


def update(momentum, gradient, weight, basis, scale, parts, squares):
    rows, cols = momentum.shape
    block = pl.BlockSpec((rows, WIDE), lambda i: (0, i))
    whole = lambda a: pl.BlockSpec(a.shape, lambda i: (0, 0))
    return pl.pallas_call(
        update_kernel,
        grid=(cols // WIDE,),
        out_shape=[shape((rows, cols)), shape((cols, RANK), bf16), shape((rows, cols), bf16)],
        in_specs=[block, block, block, whole(basis), whole(scale)] + [whole(a) for a in parts + squares],
        out_specs=[block, pl.BlockSpec((WIDE, RANK), lambda i: (i, 0)), block],
        scratch_shapes=[pltpu.VMEM((cols, RANK), bf16), pltpu.VMEM((4 * rows, RANK), bf16)],
        compiler_params=pltpu.CompilerParams(vmem_limit_bytes=40 * 1024 * 1024),
        cost_estimate=pl.CostEstimate(flops=8 * rows * cols * RANK, bytes_accessed=16 * rows * cols, transcendentals=0),
    )(momentum, gradient, weight, basis, scale, *parts, *squares)


def over_z(a):
    return lax.all_to_all(a, "dp", 0, 0, axis_index_groups=Z_GROUPS, tiled=True)


def shards(momentum, gradient, factor, weight):
    rows, cols = momentum.shape

    flipped, given, kept = project(momentum, gradient, factor)
    blocks = lax.all_to_all(flipped, "dp", 0, 0, axis_index_groups=Y_GROUPS, tiled=True)
    pair = kept + lax.ppermute(given, "tensor", OTHER_CORE)
    xs = [pair] + [lax.ppermute(pair, "tensor", from_x(k)) for k in range(1, NX)]
    mine = (xs[0] + xs[2]) + (xs[1] + xs[3])
    mine = [mine] + [lax.ppermute(mine, "dp", from_y(k)) for k in range(1, NY)]

    gram_given, gram_kept, stacked = gram_halves(mine)
    gram_pair = gram_kept + lax.ppermute(gram_given, "tensor", OTHER_CORE)
    stacked, blocks = lax.optimization_barrier((stacked, blocks))
    other = lax.ppermute(stacked, "tensor", OTHER_CORE)

    right_kept, right_a, right_b, projected = right_sums(stacked, other, blocks)
    right_a = lax.ppermute(right_a, "dp", to_neighbour(0))
    right_b = lax.ppermute(right_b, "dp", to_neighbour(1))
    gram_shares = share(over_z(gram_pair))
    gram_shares, right_a, right_b = lax.optimization_barrier((gram_shares, right_a, right_b))
    pairs = shifted(right_kept, right_a, right_b)
    pairs = [pairs[0]] + [lax.ppermute(pairs[k], "dp", from_z(NZ - 2 * k)) for k in range(1, NZ // 2)]
    gram_half = over_z(gram_shares)
    gram_other = lax.ppermute(gram_half, "tensor", OTHER_CORE)
    right0 = spread_sum(pairs)
    inverse = inverse_cholesky(gram_half, gram_other, right0)
    right0 = over_z(right0)

    sent, squares, basis = normalised(right0, projected, inverse)
    sent = sent.astype(jnp.float16)
    sent_y = [sent] + [lax.ppermute(sent, "dp", from_y(k)) for k in range(1, NY)]
    squares_x = [squares] + [lax.ppermute(squares, "tensor", from_x(k)) for k in range(1, NX)]
    total = (squares_x[0] + squares_x[2]) + (squares_x[1] + squares_x[3])
    total = total + lax.ppermute(total, "tensor", OTHER_CORE)
    both = jnp.concatenate([squares, total], 0)
    both_y = [both] + [lax.ppermute(both, "dp", from_y(k)) for k in range(1, NY)]
    both_y, sent_y = lax.optimization_barrier((both_y, sent_y))
    total = (both_y[0][1:] + both_y[2][1:]) + (both_y[1][1:] + both_y[3][1:])
    scale = jnp.sqrt(total / (cols * 2 * NX) + epsilon)
    sent_y = [a.astype(f32) for a in sent_y]
    return update(momentum, gradient, weight, basis, scale, sent_y, both_y)


def solution(mesh):
    in_specs = (P("dp", "tensor"), P("dp", "tensor"), P("tensor", None), P("dp", "tensor"))
    out_specs = (P("dp", "tensor"), P("tensor", None), P("dp", "tensor"))
    return jax.shard_map(shards, mesh=mesh, in_specs=in_specs, out_specs=out_specs, check_vma=False)
```
